768 devices in a mesh: rep: 12 (over z), dp: 16 (over y, core), tp: 4 (over x).
Axes of the slice: x: 4, y: 8, z: 12, core: 2. Of those that a mesh axis runs over, the one named last changes fastest.
Arguments:
- hidden_in: bfloat16 [73728, 8192], P(('rep', 'dp')), may hold values from -0.022094727 to 0.022094727
- value_grad: bfloat16 [73728, 512], P(('rep', 'dp'), 'tp'), may hold values from -6 to 6
- weight_shards: bfloat16 [12288, 512], P('dp', 'tp'), may hold values from -0.25 to 0.25
- shard_blocks: int32 [16], replicated, may hold values from 1 to 6, as said below
- token_counts: int32 [192], P(('rep', 'dp')), may hold values from 96 to 384, as said below
Outputs:
- input_grad: bfloat16 [73728, 8192], P(('rep', 'dp'), 'tp')
- weight_grad: float32 [12288, 512], P('dp', 'tp')
The draws below stay inside these ranges and needn't reach their ends.
Inputs may be any that keep to these rules, and one draw needn't show every extreme that they name: `shard_blocks`: sums to 64; some owner holds exactly 6 blocks. `token_counts`: some micro-batch is full and some holds exactly 96 tokens.
All inputs are finite; a program needn't handle non-finite values.
Results may differ from the reference program's by a relative error of at most 0.013.
Values may be sent and summed in bfloat16 or wider, within the bound.
No kernel may reach another device: no remote copies, remote signals or barrier semaphores. Data moves between devices by JAX's collectives and lax.ppermute only.
A program may use at most 128 MiB of HBM per device.

```python
import jax
import jax.numpy as jnp
from jax import lax

D = 8192
HEAD = 128
BLOCK = 128
TOK_DEV = 384
KVW = 512
BLK_MEAN = 4
SHARD_ROWS = 768
TOKENS = 73728
N_REP = 12
N_DP = 16
N_TP = 4


def draw_shard_blocks(key, part):
    key = jax.random.fold_in(key, 11)
    rank = jax.random.permutation(key, N_DP)
    extra = BLK_MEAN // 2
    others = N_DP - 1
    loss = extra // others + (rank - 1 < extra % others).astype(jnp.int32)
    loss = jnp.where(rank == 0, 0, loss)
    blocks = BLK_MEAN - loss + jnp.where(rank == 0, extra, 0)
    return blocks.astype(jnp.int32)


def draw_token_counts(key, part):
    key = jax.random.fold_in(key, 12)
    first, second = jax.random.split(key)
    total = N_REP * N_DP
    counts = jax.random.randint(first, (total,), TOK_DEV // 4, TOK_DEV + 1)
    rank = jax.random.permutation(second, total)
    counts = jnp.where(rank == 0, TOK_DEV, jnp.where(rank == 1, TOK_DEV // 4, counts))
    return counts.astype(jnp.int32)


def level_of(stream_key, extent, cuts, smallest, top_value):
    factor_of = 1.0
    for axis_at, parts in cuts:
        heights = jax.random.uniform(jax.random.fold_in(jax.random.fold_in(stream_key, 6), axis_at), (parts,), jnp.float32, smallest / len(cuts), top_value / len(cuts))
        factor_of = factor_of * jnp.repeat(jnp.exp(heights), extent[axis_at] // parts).reshape((-1,) + (1,) * (len(extent) - 1 - axis_at))
    return factor_of


def normal_values(stream_key, extent, spread, most, cuts=(), held_as=jnp.bfloat16):
    entries = jax.random.normal(stream_key, extent, jnp.float32) * spread
    if len(cuts) > 0:
        entries = level_of(stream_key, extent, cuts, -0.22, 0.18) * entries
    return jnp.clip(entries, min=-most, max=most).astype(held_as)


def setup_inputs(seed: int = 0) -> dict:
    key_list = jax.random.split(jax.random.key(seed), 6)
    hidden_in = normal_values(key_list[0], (TOKENS, D), (TOKENS ** -0.5), 0.022094727, ((0, 192),))
    value_grad = normal_values(key_list[1], (TOKENS, KVW), 1.0, 6.0, ((0, 192), (1, 4)))
    weight_shards = normal_values(key_list[2], (N_DP * SHARD_ROWS, KVW), KVW ** -0.5, 0.25, ((0, 16), (1, 4)))
    shard_blocks = draw_shard_blocks(jax.random.fold_in(key_list[5], 71), 0)
    token_counts = draw_token_counts(jax.random.fold_in(key_list[5], 71), 0)
    return {"hidden_in": hidden_in, "value_grad": value_grad, "weight_shards": weight_shards, "shard_blocks": shard_blocks, "token_counts": token_counts}


def reference(hidden_in, value_grad, weight_shards, shard_blocks, token_counts):
    lengths = (shard_blocks * BLOCK).astype(jnp.int32)
    starts = (jnp.cumsum(lengths) - lengths).astype(jnp.int32)
    rows = jnp.arange(D, dtype=jnp.int32)
    owner = jnp.sum((rows[:, None] >= (starts + lengths)[None, :]).astype(jnp.int32), axis=1).astype(jnp.int32)
    source = (owner * SHARD_ROWS + rows - starts[owner]).astype(jnp.int32)
    weight = weight_shards[source]
    batches = TOKENS // TOK_DEV
    live = jnp.arange(TOK_DEV, dtype=jnp.int32)[None, :] < token_counts[:, None]
    grads = value_grad.reshape(batches, TOK_DEV, KVW)
    masked = jnp.where(live[:, :, None], grads, jnp.zeros_like(grads))
    inputs = hidden_in.reshape(batches, TOK_DEV, D)

    def rows_out(block):
        total = jnp.zeros((TOK_DEV, D), jnp.float32)
        for head in range(N_TP):
            part = jnp.dot(block[:, head * HEAD:(head + 1) * HEAD], weight[:, head * HEAD:(head + 1) * HEAD].T,
                           preferred_element_type=jnp.float32)
            total = total + part.astype(jnp.bfloat16).astype(jnp.float32)
        return total.astype(jnp.bfloat16)

    input_grad = lax.map(rows_out, masked).reshape(TOKENS, D)

    def accumulate(total, pair):
        activ, block = pair
        part = jnp.dot(activ.T, block, preferred_element_type=jnp.float32)
        return total + part, None

    full, _ = lax.scan(accumulate, jnp.zeros((D, KVW), jnp.float32), (inputs, masked))
    place = jnp.arange(N_DP * SHARD_ROWS, dtype=jnp.int32)
    slot_owner = (place // SHARD_ROWS).astype(jnp.int32)
    inner = (place % SHARD_ROWS).astype(jnp.int32)
    valid = inner < lengths[slot_owner]
    column = jnp.minimum(starts[slot_owner] + inner, D - 1).astype(jnp.int32)
    weight_grad = jnp.where(valid[:, None], full[column], jnp.zeros((), jnp.float32))
    return input_grad, weight_grad
```

```python
import functools

import jax
import jax.numpy as jnp
from jax import lax
from jax.experimental import pallas as pl
from jax.experimental.pallas import tpu as pltpu
from jax.sharding import PartitionSpec as P

BLOCK = 128
SPLIT = 3
PIECE = 48
PIECE_AT = (0, 48, 80)
BIG_VMEM = 58 * 1024 * 1024
SMALL = pltpu.CompilerParams(vmem_limit_bytes=12 * 1024 * 1024)


def fill_places(blocks_ref, place, slot_blocks):
    def owner_places(owner, first):
        def one(at, carry):
            place[first + at] = owner * slot_blocks + at
            return carry

        lax.fori_loop(0, blocks_ref[owner], one, 0)
        return first + blocks_ref[owner]

    lax.fori_loop(0, blocks_ref.shape[0], owner_places, 0)


def grad_kernel(per_step, slot_blocks, counts_ref, blocks_ref, hidden_ref, grad_ref, send_ref, keep_ref, place, masked_t):
    step = pl.program_id(0)
    core = lax.rem(lax.axis_index("dp"), 2)
    turn = lax.rem(lax.axis_index("rep"), SPLIT)
    owners = blocks_ref.shape[0]
    part_blocks = slot_blocks // SPLIT

    @pl.when(step == 0)
    def _():
        fill_places(blocks_ref, place, slot_blocks)
        send_ref[...] = jnp.zeros_like(send_ref)
        keep_ref[...] = jnp.zeros_like(keep_ref)
        live = lax.broadcasted_iota(jnp.int32, grad_ref.shape, 0) < counts_ref[0]
        masked = jnp.where(live, grad_ref[...].astype(jnp.float32), 0.0)
        masked_t[...] = masked.T.astype(masked_t.dtype)

    product = jnp.dot(masked_t[...], hidden_ref[...], preferred_element_type=jnp.float32)
    for at in range(per_step):
        slot = place[step * per_step + at]
        owner = lax.div(slot, slot_blocks)
        inside = lax.rem(slot, slot_blocks)
        part = lax.rem(lax.div(inside, part_blocks) + SPLIT - turn, SPLIT)
        block = (part * (owners // 2) + lax.div(owner, 2)) * part_blocks + lax.rem(inside, part_blocks)
        row = pl.multiple_of(block * BLOCK, BLOCK)
        tile = product[:, at * BLOCK:(at + 1) * BLOCK].astype(send_ref.dtype)
        mine = lax.rem(owner, 2) == core

        @pl.when(mine)
        def _():
            keep_ref[pl.ds(row, BLOCK), :] = tile

        @pl.when(jnp.logical_not(mine))
        def _():
            send_ref[pl.ds(row, BLOCK), :] = tile


def grad_products(counts, shard_blocks, hidden, grad, slot_rows):
    rows, width = hidden.shape
    owners = shard_blocks.shape[0]
    chunk = 1024
    half = (owners // 2) * slot_rows
    out = jax.ShapeDtypeStruct((half, grad.shape[1]), jnp.bfloat16)
    return pl.pallas_call(
        functools.partial(grad_kernel, chunk // BLOCK, slot_rows // BLOCK),
        grid=(width // chunk,),
        in_specs=[
            pl.BlockSpec(memory_space=pltpu.SMEM),
            pl.BlockSpec(memory_space=pltpu.SMEM),
            pl.BlockSpec((rows, chunk), lambda i: (0, i)),
            pl.BlockSpec(grad.shape, lambda i: (0, 0)),
        ],
        out_specs=[pl.BlockSpec(out.shape, lambda i: (0, 0))] * 2,
        out_shape=[out, out],
        scratch_shapes=[
            pltpu.SMEM((width // BLOCK,), jnp.int32),
            pltpu.VMEM((grad.shape[1], rows), jnp.bfloat16),
        ],
        compiler_params=pltpu.CompilerParams(vmem_limit_bytes=BIG_VMEM),
        cost_estimate=pl.CostEstimate(
            flops=2 * rows * width * grad.shape[1], bytes_accessed=2 * rows * width + 4 * half * 128, transcendentals=0
        ),
        name="grad_products",
    )(counts, shard_blocks, hidden, grad)


def pair_kernel(keep_ref, received_ref, *outs):
    rows = outs[0].shape[0]
    for k, out in enumerate(outs):
        here = pl.ds(k * rows, rows)
        total = keep_ref[here, :].astype(jnp.float32) + received_ref[here, :].astype(jnp.float32)
        out[...] = total.astype(out.dtype)


def paired_parts(keep, received):
    out = jax.ShapeDtypeStruct((keep.shape[0] // SPLIT, keep.shape[1]), keep.dtype)
    return pl.pallas_call(pair_kernel, out_shape=[out] * SPLIT, compiler_params=SMALL, name="pair_parts")(keep, received)


def summed(parts):
    total = parts[0].astype(jnp.float32)
    for part in parts[1:]:
        total = total + part.astype(jnp.float32)
    return total.astype(parts[0].dtype)


def finish_kernel(share, total_ref, out_ref):
    n_rep = total_ref.shape[0] // share
    per = out_ref.shape[0] // SPLIT
    rows = [None] * (out_ref.shape[0] // share)
    for rep in range(n_rep):
        first = (rep % SPLIT) * per + (rep // SPLIT) * share
        rows[first // share] = total_ref[rep * share:(rep + 1) * share, :].astype(out_ref.dtype)
    slot = jnp.concatenate(rows, axis=0)
    for at in range(out_ref.shape[0] // BLOCK):
        out_ref[at * BLOCK:(at + 1) * BLOCK, :] = slot[at * BLOCK:(at + 1) * BLOCK, :].T


def finished(total, share):
    return pl.pallas_call(
        functools.partial(finish_kernel, share),
        out_shape=jax.ShapeDtypeStruct(total.shape, jnp.float32),
        compiler_params=SMALL,
        name="finish_weight_grad",
    )(total)


def compact_kernel(slot_blocks, n_tp, blocks_ref, mine_ref, other_ref, grad_ref, out_ref, place):
    core = lax.rem(lax.axis_index("dp"), 2)
    fill_places(blocks_ref, place, slot_blocks)
    per = place.shape[0] // n_tp
    for target in range(n_tp):
        def one(at, carry):
            slot = place[target * per + at]
            owner = lax.div(slot, slot_blocks)
            block = lax.div(owner, 2) * slot_blocks + lax.rem(slot, slot_blocks)
            source = pl.ds(pl.multiple_of(block * PIECE, 16), PIECE)
            here = pl.ds(pl.multiple_of(at * PIECE, 16), PIECE)
            mine = lax.rem(owner, 2) == core

            @pl.when(mine)
            def _():
                out_ref[target, here, :] = mine_ref[source, :]

            @pl.when(jnp.logical_not(mine))
            def _():
                out_ref[target, here, :] = other_ref[source, :]

            return carry

        lax.fori_loop(0, per, one, 0)
        out_ref[target, pl.ds(per * PIECE, grad_ref.shape[0]), :] = grad_ref[...]


def compacted(shard_blocks, mine, other, grad, slot_rows, n_tp, width):
    n_blocks = width // BLOCK
    rows = n_blocks // n_tp * PIECE + grad.shape[0]
    return pl.pallas_call(
        functools.partial(compact_kernel, slot_rows // BLOCK, n_tp),
        in_specs=[pl.BlockSpec(memory_space=pltpu.SMEM)] + [pl.BlockSpec(memory_space=pltpu.VMEM)] * 3,
        out_shape=jax.ShapeDtypeStruct((n_tp, rows, grad.shape[1]), grad.dtype),
        scratch_shapes=[pltpu.SMEM((n_blocks,), jnp.int32)],
        compiler_params=SMALL,
        name="compact_rows",
    )(shard_blocks, mine, other, grad)


def input_kernel(counts_ref, own_ref, before_ref, after_ref, grads_ref, out_ref, masked, weight):
    step = pl.program_id(0)
    turn = lax.rem(lax.axis_index("rep"), SPLIT)
    heads = own_ref.shape[0]
    blocks = own_ref.shape[1] // PIECE

    @pl.when(step == 0)
    def _():
        for h in range(heads):
            grad = grads_ref[h].astype(jnp.float32)
            live = lax.broadcasted_iota(jnp.int32, grad.shape, 0) < counts_ref[0]
            masked[:, h * BLOCK:(h + 1) * BLOCK] = jnp.where(live, grad, 0.0).astype(masked.dtype)

    for own in range(SPLIT):
        @pl.when(turn == own)
        def _():
            for shift, ref in ((0, own_ref), (SPLIT - 1, before_ref), (1, after_ref)):
                piece = (own + shift) % SPLIT
                first = PIECE_AT[piece]
                for h in range(heads):
                    for b in range(blocks):
                        weight[b * BLOCK + first:b * BLOCK + first + PIECE, h * BLOCK:(h + 1) * BLOCK] = ref[
                            h, b * PIECE:(b + 1) * PIECE, :
                        ]

    out_ref[...] = lax.dot_general(
        masked[...], weight[...], (((1,), (1,)), ((), ())), preferred_element_type=jnp.float32
    ).astype(out_ref.dtype)


def input_product(counts, own, before, after, rows_dev):
    n_tp, _, head = own.shape
    pieces = before.shape[1]
    steps = 4
    blocks = pieces // PIECE // steps
    chunk = blocks * BLOCK
    piece = pl.BlockSpec((n_tp, blocks * PIECE, head), lambda i: (0, i, 0))
    return pl.pallas_call(
        input_kernel,
        grid=(steps,),
        in_specs=[
            pl.BlockSpec(memory_space=pltpu.SMEM),
            piece,
            piece,
            piece,
            pl.BlockSpec((n_tp, rows_dev, head), lambda i: (0, pieces // rows_dev, 0)),
        ],
        out_specs=pl.BlockSpec((rows_dev, chunk), lambda i: (0, i)),
        out_shape=jax.ShapeDtypeStruct((rows_dev, steps * chunk), jnp.bfloat16),
        scratch_shapes=[
            pltpu.VMEM((rows_dev, head * n_tp), jnp.bfloat16),
            pltpu.VMEM((chunk, head * n_tp), jnp.bfloat16),
        ],
        compiler_params=pltpu.CompilerParams(vmem_limit_bytes=24 * 1024 * 1024),
        cost_estimate=pl.CostEstimate(
            flops=2 * rows_dev * steps * chunk * head * n_tp,
            bytes_accessed=2 * steps * chunk * (head * n_tp + rows_dev),
            transcendentals=0,
        ),
        name="input_grad",
    )(counts, own, before, after, own)


def on_device(hidden_in, value_grad, weight_shards, shard_blocks, token_counts):
    rows_dev, width = hidden_in.shape
    slot_rows, head = weight_shards.shape
    n_dp, n_tp, n_rep = lax.axis_size("dp"), lax.axis_size("tp"), lax.axis_size("rep")
    n_y = n_dp // 2
    slot_blocks = slot_rows // BLOCK
    core_swap = [(i, i ^ 1) for i in range(n_dp)]
    along_y = [[c + 2 * y for y in range(n_y)] for c in range(2)]
    up = [(i, (i + 1) % n_rep) for i in range(n_rep)]
    down = [(i, (i - 1) % n_rep) for i in range(n_rep)]

    turn = lax.rem(lax.axis_index("rep"), SPLIT)
    first = turn * PIECE_AT[1] - jnp.where(turn == 2, 2 * PIECE_AT[1] - PIECE_AT[2], 0)
    piece = lax.dynamic_slice_in_dim(weight_shards.reshape(slot_blocks, BLOCK, head), first, PIECE, 1)
    piece = piece.reshape(1, slot_blocks * PIECE, head)
    held = lax.all_to_all(
        jnp.broadcast_to(piece, (n_y,) + piece.shape[1:]), "dp", 0, 0, axis_index_groups=along_y
    ).reshape(n_y * slot_blocks * PIECE, head)
    other = lax.ppermute(held, "dp", core_swap)
    sent = compacted(shard_blocks, held, other, value_grad, slot_rows, n_tp, width)
    own = lax.all_to_all(sent, "tp", 0, 0)
    pieces = own[:, : own.shape[1] - rows_dev]
    before = lax.ppermute(pieces, "rep", up)
    after = lax.ppermute(pieces, "rep", down)
    input_grad = input_product(token_counts, own, before, after, rows_dev)

    send, keep = grad_products(token_counts, shard_blocks, hidden_in, value_grad, slot_rows)
    received = lax.ppermute(send, "dp", core_swap)
    stay, to_next, to_last = paired_parts(keep, received)
    part = summed([stay, lax.ppermute(to_next, "rep", up), lax.ppermute(to_last, "rep", down)])
    spread = lax.all_to_all(part.reshape(n_y, slot_rows // SPLIT, head), "dp", 0, 0, axis_index_groups=along_y)
    owned = summed([spread[y] for y in range(n_y)])
    fellows = [[k + SPLIT * q for q in range(n_rep // SPLIT)] for k in range(SPLIT)]
    share_rows = slot_rows // n_rep
    shares = lax.all_to_all(
        owned.reshape(n_rep // SPLIT, share_rows, head), "rep", 0, 0, axis_index_groups=fellows
    )
    share = summed([shares[q] for q in range(n_rep // SPLIT)])
    total = lax.all_to_all(jnp.broadcast_to(share[None], (n_rep,) + share.shape), "rep", 0, 0)
    weight_grad = finished(total.reshape(slot_rows, head), share_rows)
    return (input_grad, weight_grad)


def solution(mesh):
    placed = (P(("rep", "dp"), None), P(("rep", "dp"), "tp"), P("dp", "tp"), P(), P(("rep", "dp")))
    return jax.shard_map(
        on_device,
        mesh=mesh,
        in_specs=placed,
        out_specs=(P(("rep", "dp"), "tp"), P("dp", "tp")),
        check_vma=False,
    )
```

```python
import functools

import jax
import jax.numpy as jnp
from jax import lax
from jax.experimental import pallas as pl
from jax.experimental.pallas import tpu as pltpu
from jax.sharding import PartitionSpec as P

BLOCK = 128
SPLIT = 3
PIECE = 48
PIECE_AT = (0, 48, 80)
SMALL = pltpu.CompilerParams(vmem_limit_bytes=12 * 1024 * 1024)


def fill_places(blocks_ref, place, slot_blocks, code):
    first = 0
    for owner in range(blocks_ref.shape[0]):
        for at in range(slot_blocks):
            place[first + at] = code(owner, at)
        first = first + blocks_ref[owner]


def grad_kernel(
    chunk, slot_blocks, counts_ref, blocks_ref, hidden_ref, grad_ref, send_ref, keep_ref, place, masked_t, chunks, sems
):
    steps = hidden_ref.shape[1] // chunk

    def load(step):
        return pltpu.make_async_copy(
            hidden_ref.at[:, pl.ds(step * chunk, chunk)], chunks.at[step], sems.at[step]
        )

    for step in range(steps):
        load(step).start()
    core = lax.rem(lax.axis_index("dp"), 2)
    turn = lax.rem(lax.axis_index("rep"), SPLIT)
    half = send_ref.shape[0]
    part_blocks = slot_blocks // SPLIT
    part_first = [lax.rem(part + SPLIT - turn, SPLIT) * (half // SPLIT) for part in range(SPLIT)]
    side = [jnp.where(core == parity, 0, half) for parity in range(2)]

    def code(owner, at):
        row = ((owner // 2) * part_blocks + at % part_blocks) * BLOCK
        return part_first[at // part_blocks] + side[owner % 2] + row

    fill_places(blocks_ref, place, slot_blocks, code)
    send_ref[...] = jnp.zeros_like(send_ref)
    keep_ref[...] = jnp.zeros_like(keep_ref)
    live = lax.broadcasted_iota(jnp.int32, grad_ref.shape, 0) < counts_ref[0]
    masked = jnp.where(live, grad_ref[...].astype(jnp.float32), 0.0)
    masked_t[...] = masked.T.astype(masked_t.dtype)

    def one(step, carry):
        load(step).wait()
        product = jnp.dot(masked_t[...], chunks[step], preferred_element_type=jnp.float32)
        for at in range(chunk // BLOCK):
            row = place[step * (chunk // BLOCK) + at]
            tile = product[:, at * BLOCK:(at + 1) * BLOCK].astype(send_ref.dtype)

            @pl.when(row < half)
            def _():
                keep_ref[pl.ds(pl.multiple_of(row, BLOCK), BLOCK), :] = tile

            @pl.when(row >= half)
            def _():
                send_ref[pl.ds(pl.multiple_of(row - half, BLOCK), BLOCK), :] = tile

        return carry

    lax.fori_loop(0, steps, one, 0)


def grad_products(counts, shard_blocks, hidden, grad, slot_rows):
    rows, width = hidden.shape
    owners = shard_blocks.shape[0]
    chunk = 1024
    steps = width // chunk
    half = (owners // 2) * slot_rows
    slot_blocks = slot_rows // BLOCK
    out = jax.ShapeDtypeStruct((half, grad.shape[1]), jnp.bfloat16)
    vmem = pl.BlockSpec(memory_space=pltpu.VMEM)
    return pl.pallas_call(
        functools.partial(grad_kernel, chunk, slot_blocks),
        in_specs=[
            pl.BlockSpec(memory_space=pltpu.SMEM),
            pl.BlockSpec(memory_space=pltpu.SMEM),
            pl.BlockSpec(memory_space=pltpu.HBM),
            vmem,
        ],
        out_specs=[vmem, vmem],
        out_shape=[out, out],
        scratch_shapes=[
            pltpu.SMEM((width // BLOCK + slot_blocks,), jnp.int32),
            pltpu.VMEM((grad.shape[1], rows), jnp.bfloat16),
            pltpu.VMEM((steps, rows, chunk), jnp.bfloat16),
            pltpu.SemaphoreType.DMA((steps,)),
        ],
        compiler_params=pltpu.CompilerParams(vmem_limit_bytes=59 * 1024 * 1024),
        cost_estimate=pl.CostEstimate(
            flops=2 * rows * width * grad.shape[1], bytes_accessed=2 * rows * width + 4 * half * 128, transcendentals=0
        ),
        name="grad_products",
    )(counts, shard_blocks, hidden, grad)


def pair_kernel(keep_ref, received_ref, *outs):
    rows = outs[0].shape[0]
    for k, out in enumerate(outs):
        here = pl.ds(k * rows, rows)
        total = keep_ref[here, :].astype(jnp.float32) + received_ref[here, :].astype(jnp.float32)
        out[...] = total.astype(out.dtype)


def paired_parts(keep, received):
    out = jax.ShapeDtypeStruct((keep.shape[0] // SPLIT, keep.shape[1]), keep.dtype)
    return pl.pallas_call(pair_kernel, out_shape=[out] * SPLIT, compiler_params=SMALL, name="pair_parts")(keep, received)


def summed(parts):
    total = parts[0].astype(jnp.float32)
    for part in parts[1:]:
        total = total + part.astype(jnp.float32)
    return total.astype(parts[0].dtype)


def finish_kernel(share, total_ref, out_ref):
    n_rep = total_ref.shape[0] // share
    per = out_ref.shape[0] // SPLIT
    rows = [None] * (out_ref.shape[0] // share)
    for rep in range(n_rep):
        first = (rep % SPLIT) * per + (rep // SPLIT) * share
        rows[first // share] = total_ref[rep * share:(rep + 1) * share, :].astype(out_ref.dtype)
    slot = jnp.concatenate(rows, axis=0)
    for at in range(out_ref.shape[0] // BLOCK):
        out_ref[at * BLOCK:(at + 1) * BLOCK, :] = slot[at * BLOCK:(at + 1) * BLOCK, :].T


def finished(total, share):
    return pl.pallas_call(
        functools.partial(finish_kernel, share),
        out_shape=jax.ShapeDtypeStruct(total.shape, jnp.float32),
        compiler_params=SMALL,
        name="finish_weight_grad",
    )(total)


def compact_kernel(slot_blocks, n_tp, blocks_ref, held_ref, grad_ref, *rest):
    outs, place = rest[:n_tp], rest[n_tp]
    index = lax.axis_index("tp")
    half = held_ref.shape[0] // 2
    fill_places(
        blocks_ref, place, slot_blocks,
        lambda owner, at: (owner % 2) * half + ((owner // 2) * slot_blocks + at) * PIECE,
    )
    per = (outs[0].shape[0] - grad_ref.shape[0]) // PIECE
    for k, out_ref in enumerate(outs):
        first = lax.rem(index + k, n_tp) * per
        for at in range(per):
            source = pl.multiple_of(place[first + at], 16)
            out_ref[at * PIECE:(at + 1) * PIECE, :] = held_ref[pl.ds(source, PIECE), :]
        out_ref[per * PIECE:, :] = grad_ref[...]


def compacted(shard_blocks, held, grad, slot_rows, n_tp, width):
    n_blocks = width // BLOCK
    slot_blocks = slot_rows // BLOCK
    rows = n_blocks // n_tp * PIECE + grad.shape[0]
    vmem = pl.BlockSpec(memory_space=pltpu.VMEM)
    return pl.pallas_call(
        functools.partial(compact_kernel, slot_blocks, n_tp),
        in_specs=[pl.BlockSpec(memory_space=pltpu.SMEM), vmem, vmem],
        out_specs=[vmem] * n_tp,
        out_shape=[jax.ShapeDtypeStruct((rows, grad.shape[1]), grad.dtype)] * n_tp,
        scratch_shapes=[pltpu.SMEM((n_blocks + slot_blocks,), jnp.int32)],
        compiler_params=SMALL,
        cost_estimate=pl.CostEstimate(flops=0, bytes_accessed=2 * rows * grad.shape[1], transcendentals=0),
        name="compact_rows",
    )(shard_blocks, held.reshape(-1, held.shape[-1]), grad)


def input_kernel(heads, counts_ref, *refs):
    own, (before_ref, after_ref), grads = refs[:heads], refs[heads:heads + 2], refs[heads + 2:2 * heads + 2]
    out_ref, masked, weight = refs[2 * heads + 2:]
    step = pl.program_id(0)
    turn = lax.rem(lax.axis_index("rep"), SPLIT)
    blocks = before_ref.shape[1] // PIECE

    @pl.when(step == 0)
    def _():
        for h in range(heads):
            grad = grads[h][...].astype(jnp.float32)
            live = lax.broadcasted_iota(jnp.int32, grad.shape, 0) < counts_ref[0]
            masked[:, h * BLOCK:(h + 1) * BLOCK] = jnp.where(live, grad, 0.0).astype(masked.dtype)

    for piece_here in range(SPLIT):
        @pl.when(turn == piece_here)
        def _():
            for shift in range(SPLIT):
                first = PIECE_AT[(piece_here + shift) % SPLIT]
                for h in range(heads):
                    ref = (own[h], after_ref.at[h], before_ref.at[h])[shift]
                    for b in range(blocks):
                        weight[b * BLOCK + first:b * BLOCK + first + PIECE, h * BLOCK:(h + 1) * BLOCK] = ref[
                            b * PIECE:(b + 1) * PIECE, :
                        ]

    out_ref[...] = lax.dot_general(
        masked[...], weight[...], (((1,), (1,)), ((), ())), preferred_element_type=jnp.float32
    ).astype(out_ref.dtype)


def input_product(counts, own, before, after, rows_dev):
    n_tp, pieces, head = before.shape
    steps = 4
    blocks = pieces // PIECE // steps
    chunk = blocks * BLOCK
    return pl.pallas_call(
        functools.partial(input_kernel, n_tp),
        grid=(steps,),
        in_specs=[pl.BlockSpec(memory_space=pltpu.SMEM)]
        + [pl.BlockSpec((blocks * PIECE, head), lambda i: (i, 0))] * n_tp
        + [pl.BlockSpec((n_tp, blocks * PIECE, head), lambda i: (0, i, 0))] * 2
        + [pl.BlockSpec((rows_dev, head), lambda i: (pieces // rows_dev, 0))] * n_tp,
        out_specs=pl.BlockSpec((rows_dev, chunk), lambda i: (0, i)),
        out_shape=jax.ShapeDtypeStruct((rows_dev, steps * chunk), jnp.bfloat16),
        scratch_shapes=[
            pltpu.VMEM((rows_dev, head * n_tp), jnp.bfloat16),
            pltpu.VMEM((chunk, head * n_tp), jnp.bfloat16),
        ],
        compiler_params=pltpu.CompilerParams(vmem_limit_bytes=16 * 1024 * 1024),
        cost_estimate=pl.CostEstimate(
            flops=2 * rows_dev * steps * chunk * head * n_tp,
            bytes_accessed=2 * steps * chunk * (head * n_tp + rows_dev),
            transcendentals=0,
        ),
        name="input_grad",
    )(counts, *own, before, after, *own)


def ordered(array, other):
    return lax.optimization_barrier((array, other))[0]


def on_device(hidden_in, value_grad, weight_shards, shard_blocks, token_counts):
    rows_dev, width = hidden_in.shape
    slot_rows, head = weight_shards.shape
    n_dp, n_tp, n_rep = lax.axis_size("dp"), lax.axis_size("tp"), lax.axis_size("rep")
    n_y = n_dp // 2
    slot_blocks = slot_rows // BLOCK
    core_swap = [(i, i ^ 1) for i in range(n_dp)]
    along_y = [[c + 2 * y for y in range(n_y)] for c in range(2)]
    up = [(i, (i + 1) % n_rep) for i in range(n_rep)]
    down = [(i, (i - 1) % n_rep) for i in range(n_rep)]

    turn = lax.rem(lax.axis_index("rep"), SPLIT)
    first = turn * PIECE_AT[1] - jnp.where(turn == 2, 2 * PIECE_AT[1] - PIECE_AT[2], 0)
    piece = lax.dynamic_slice_in_dim(weight_shards.reshape(slot_blocks, BLOCK, head), first, PIECE, 1)
    piece = piece.reshape(1, slot_blocks * PIECE, head)
    held = lax.all_to_all(
        jnp.broadcast_to(piece, (n_y,) + piece.shape[1:]), "dp", 0, 0, axis_index_groups=along_y
    ).reshape(n_y * slot_blocks * PIECE, head)
    send, keep = grad_products(token_counts, shard_blocks, hidden_in, value_grad, slot_rows)
    received = lax.ppermute(send, "dp", core_swap)
    stay, to_next, to_last = paired_parts(keep, received)

    pair = [[2 * y, 2 * y + 1] for y in range(n_y)]
    held = lax.all_to_all(jnp.broadcast_to(held[None], (2,) + held.shape), "dp", 0, 0, axis_index_groups=pair)
    sent = compacted(shard_blocks, held, value_grad, slot_rows, n_tp, width)
    own = [sent[0]] + [
        lax.ppermute(sent[k], "tp", [(i, (i + k) % n_tp) for i in range(n_tp)]) for k in range(1, n_tp)
    ]
    pieces = jnp.stack([part[: part.shape[0] - rows_dev] for part in own])
    before = lax.ppermute(pieces, "rep", up)
    after = lax.ppermute(pieces, "rep", down)
    input_grad = input_product(token_counts, own, before, after, rows_dev)

    stay = ordered(stay, sent[0])
    part = summed([stay, lax.ppermute(to_next, "rep", up), lax.ppermute(to_last, "rep", down)])
    spread = lax.all_to_all(part.reshape(n_y, slot_rows // SPLIT, head), "dp", 0, 0, axis_index_groups=along_y)
    owned = summed([spread[y] for y in range(n_y)])
    fellows = [[k + SPLIT * q for q in range(n_rep // SPLIT)] for k in range(SPLIT)]
    share_rows = slot_rows // n_rep
    shares = lax.all_to_all(
        owned.reshape(n_rep // SPLIT, share_rows, head), "rep", 0, 0, axis_index_groups=fellows
    )
    share = summed([shares[q] for q in range(n_rep // SPLIT)])
    total = lax.all_to_all(jnp.broadcast_to(share[None], (n_rep,) + share.shape), "rep", 0, 0)
    weight_grad = finished(total.reshape(slot_rows, head), share_rows)
    return (input_grad, weight_grad)


def solution(mesh):
    placed = (P(("rep", "dp"), None), P(("rep", "dp"), "tp"), P("dp", "tp"), P(), P(("rep", "dp")))
    return jax.shard_map(
        on_device,
        mesh=mesh,
        in_specs=placed,
        out_specs=(P(("rep", "dp"), "tp"), P("dp", "tp")),
        check_vma=False,
    )
```

```python
import functools

import jax
import jax.numpy as jnp
from jax import lax
from jax.experimental import pallas as pl
from jax.experimental.pallas import tpu as pltpu
from jax.sharding import PartitionSpec as P

BLOCK = 128
SPLIT = 3
SMALL = pltpu.CompilerParams(vmem_limit_bytes=12 * 1024 * 1024)


def fill_places(blocks_ref, place, slot_blocks, code):
    first = 0
    for owner in range(blocks_ref.shape[0]):
        for at in range(slot_blocks):
            place[first + at] = code(owner, at)
        first = first + blocks_ref[owner]


def grad_kernel(
    chunk, slot_blocks, counts_ref, blocks_ref, hidden_ref, grad_ref, send_ref, keep_ref, place, masked_t, chunks, sems
):
    steps = hidden_ref.shape[1] // chunk

    def load(step):
        return pltpu.make_async_copy(
            hidden_ref.at[:, pl.ds(step * chunk, chunk)], chunks.at[step], sems.at[step]
        )

    for step in range(steps):
        load(step).start()
    core = lax.rem(lax.axis_index("dp"), 2)
    turn = lax.rem(lax.axis_index("rep"), SPLIT)
    half = send_ref.shape[0]
    part_blocks = slot_blocks // SPLIT
    part_first = [lax.rem(part + SPLIT - turn, SPLIT) * (half // SPLIT) for part in range(SPLIT)]
    side = [jnp.where(core == parity, 0, half) for parity in range(2)]

    def code(owner, at):
        row = ((owner // 2) * part_blocks + at % part_blocks) * BLOCK
        return part_first[at // part_blocks] + side[owner % 2] + row

    fill_places(blocks_ref, place, slot_blocks, code)
    send_ref[...] = jnp.zeros_like(send_ref)
    keep_ref[...] = jnp.zeros_like(keep_ref)
    live = lax.broadcasted_iota(jnp.int32, grad_ref.shape, 0) < counts_ref[0]
    masked = jnp.where(live, grad_ref[...].astype(jnp.float32), 0.0)
    masked_t[...] = masked.T.astype(masked_t.dtype)

    def one(step, carry):
        load(step).wait()
        product = jnp.dot(masked_t[...], chunks[step], preferred_element_type=jnp.float32)
        for at in range(chunk // BLOCK):
            row = place[step * (chunk // BLOCK) + at]
            tile = product[:, at * BLOCK:(at + 1) * BLOCK].astype(send_ref.dtype)

            @pl.when(row < half)
            def _():
                keep_ref[pl.ds(pl.multiple_of(row, BLOCK), BLOCK), :] = tile

            @pl.when(row >= half)
            def _():
                send_ref[pl.ds(pl.multiple_of(row - half, BLOCK), BLOCK), :] = tile

        return carry

    lax.fori_loop(0, steps, one, 0)


def grad_products(counts, shard_blocks, hidden, grad, slot_rows):
    rows, width = hidden.shape
    owners = shard_blocks.shape[0]
    chunk = 1024
    steps = width // chunk
    half = (owners // 2) * slot_rows
    slot_blocks = slot_rows // BLOCK
    out = jax.ShapeDtypeStruct((half, grad.shape[1]), jnp.bfloat16)
    vmem = pl.BlockSpec(memory_space=pltpu.VMEM)
    return pl.pallas_call(
        functools.partial(grad_kernel, chunk, slot_blocks),
        in_specs=[
            pl.BlockSpec(memory_space=pltpu.SMEM),
            pl.BlockSpec(memory_space=pltpu.SMEM),
            pl.BlockSpec(memory_space=pltpu.HBM),
            vmem,
        ],
        out_specs=[vmem, vmem],
        out_shape=[out, out],
        scratch_shapes=[
            pltpu.SMEM((width // BLOCK + slot_blocks,), jnp.int32),
            pltpu.VMEM((grad.shape[1], rows), jnp.bfloat16),
            pltpu.VMEM((steps, rows, chunk), jnp.bfloat16),
            pltpu.SemaphoreType.DMA((steps,)),
        ],
        compiler_params=pltpu.CompilerParams(vmem_limit_bytes=59 * 1024 * 1024),
        cost_estimate=pl.CostEstimate(
            flops=2 * rows * width * grad.shape[1], bytes_accessed=2 * rows * width + 4 * half * 128, transcendentals=0
        ),
        name="grad_products",
    )(counts, shard_blocks, hidden, grad)


def pair_kernel(keep_ref, received_ref, *outs):
    rows = outs[0].shape[0]
    for k, out in enumerate(outs):
        here = pl.ds(k * rows, rows)
        total = keep_ref[here, :].astype(jnp.float32) + received_ref[here, :].astype(jnp.float32)
        out[...] = total.astype(out.dtype)


def paired_parts(keep, received):
    out = jax.ShapeDtypeStruct((keep.shape[0] // SPLIT, keep.shape[1]), keep.dtype)
    return pl.pallas_call(pair_kernel, out_shape=[out] * SPLIT, compiler_params=SMALL, name="pair_parts")(keep, received)


def summed(parts):
    total = parts[0].astype(jnp.float32)
    for part in parts[1:]:
        total = total + part.astype(jnp.float32)
    return total.astype(parts[0].dtype)


def finish_kernel(share, total_ref, out_ref):
    n_rep = total_ref.shape[0] // share
    per = out_ref.shape[0] // SPLIT
    rows = [None] * (out_ref.shape[0] // share)
    for rep in range(n_rep):
        first = (rep % SPLIT) * per + (rep // SPLIT) * share
        rows[first // share] = total_ref[rep * share:(rep + 1) * share, :].astype(out_ref.dtype)
    slot = jnp.concatenate(rows, axis=0)
    for at in range(out_ref.shape[0] // BLOCK):
        out_ref[at * BLOCK:(at + 1) * BLOCK, :] = slot[at * BLOCK:(at + 1) * BLOCK, :].T


def finished(total, share):
    return pl.pallas_call(
        functools.partial(finish_kernel, share),
        out_shape=jax.ShapeDtypeStruct(total.shape, jnp.float32),
        compiler_params=SMALL,
        name="finish_weight_grad",
    )(total)


def compact_kernel(slot_blocks, n_tp, blocks_ref, gathered_ref, grad_ref, *rest):
    outs, place = rest[:n_tp], rest[n_tp]
    index = lax.axis_index("tp")
    fill_places(blocks_ref, place, slot_blocks, lambda owner, at: (owner * slot_blocks + at) * BLOCK)
    per = (outs[0].shape[0] - grad_ref.shape[0]) // BLOCK
    for k, out_ref in enumerate(outs):
        first = lax.rem(index + k, n_tp) * per
        for at in range(per):
            source = pl.multiple_of(place[first + at], BLOCK)
            out_ref[at * BLOCK:(at + 1) * BLOCK, :] = gathered_ref[pl.ds(source, BLOCK), :]
        out_ref[per * BLOCK:, :] = grad_ref[...]


def compacted(shard_blocks, gathered, grad, slot_rows, n_tp, width):
    slot_blocks = slot_rows // BLOCK
    rows = width // n_tp + grad.shape[0]
    vmem = pl.BlockSpec(memory_space=pltpu.VMEM)
    return pl.pallas_call(
        functools.partial(compact_kernel, slot_blocks, n_tp),
        in_specs=[pl.BlockSpec(memory_space=pltpu.SMEM), vmem, vmem],
        out_specs=[vmem] * n_tp,
        out_shape=[jax.ShapeDtypeStruct((rows, grad.shape[1]), grad.dtype)] * n_tp,
        scratch_shapes=[pltpu.SMEM((width // BLOCK + slot_blocks,), jnp.int32)],
        compiler_params=SMALL,
        cost_estimate=pl.CostEstimate(flops=0, bytes_accessed=4 * width * grad.shape[1], transcendentals=0),
        name="compact_rows",
    )(shard_blocks, gathered, grad)


def input_kernel(heads, counts_ref, *refs):
    weights, grads = refs[:heads], refs[heads:2 * heads]
    out_ref, masked = refs[2 * heads:]

    @pl.when(pl.program_id(0) == 0)
    def _():
        for h in range(heads):
            grad = grads[h][...].astype(jnp.float32)
            live = lax.broadcasted_iota(jnp.int32, grad.shape, 0) < counts_ref[0]
            masked[:, h * BLOCK:(h + 1) * BLOCK] = jnp.where(live, grad, 0.0).astype(masked.dtype)

    weight = jnp.concatenate([w[...] for w in weights], axis=1)
    out_ref[...] = lax.dot_general(
        masked[...], weight, (((1,), (1,)), ((), ())), preferred_element_type=jnp.float32
    ).astype(out_ref.dtype)


def input_product(counts, parts, rows_dev):
    n = len(parts)
    rows, head = parts[0].shape[0] - rows_dev, parts[0].shape[1]
    chunk = 512
    return pl.pallas_call(
        functools.partial(input_kernel, n),
        grid=(rows // chunk,),
        in_specs=[pl.BlockSpec(memory_space=pltpu.SMEM)]
        + [pl.BlockSpec((chunk, head), lambda i: (i, 0))] * n
        + [pl.BlockSpec((pl.Element(rows_dev), pl.Element(head)), lambda i: (rows, 0))] * n,
        out_specs=pl.BlockSpec((rows_dev, chunk), lambda i: (0, i)),
        out_shape=jax.ShapeDtypeStruct((rows_dev, rows), jnp.bfloat16),
        scratch_shapes=[pltpu.VMEM((rows_dev, head * n), jnp.bfloat16)],
        compiler_params=pltpu.CompilerParams(vmem_limit_bytes=16 * 1024 * 1024),
        cost_estimate=pl.CostEstimate(
            flops=2 * rows_dev * rows * head * n, bytes_accessed=2 * rows * (head * n + rows_dev), transcendentals=0
        ),
        name="input_grad",
    )(counts, *parts, *parts)


def on_device(hidden_in, value_grad, weight_shards, shard_blocks, token_counts):
    rows_dev, width = hidden_in.shape
    slot_rows, head = weight_shards.shape
    n_dp, n_tp, n_rep = lax.axis_size("dp"), lax.axis_size("tp"), lax.axis_size("rep")
    n_y = n_dp // 2
    core_swap = [(i, i ^ 1) for i in range(n_dp)]
    along_y = [[c + 2 * y for y in range(n_y)] for c in range(2)]
    up = [(i, (i + 1) % n_rep) for i in range(n_rep)]
    down = [(i, (i - 1) % n_rep) for i in range(n_rep)]

    gathered = lax.all_gather(weight_shards, "dp", axis=0, tiled=True)
    send, keep = grad_products(token_counts, shard_blocks, hidden_in, value_grad, slot_rows)
    received = lax.ppermute(send, "dp", core_swap)
    stay, to_next, to_last = paired_parts(keep, received)

    sent = compacted(shard_blocks, gathered, value_grad, slot_rows, n_tp, width)
    parts = [sent[0]] + [
        lax.ppermute(sent[k], "tp", [(i, (i + k) % n_tp) for i in range(n_tp)]) for k in range(1, n_tp)
    ]
    input_grad = input_product(token_counts, parts, rows_dev)

    part = summed([stay, lax.ppermute(to_next, "rep", up), lax.ppermute(to_last, "rep", down)])
    spread = lax.all_to_all(part.reshape(n_y, slot_rows // SPLIT, head), "dp", 0, 0, axis_index_groups=along_y)
    owned = summed([spread[y] for y in range(n_y)])
    fellows = [[k + SPLIT * q for q in range(n_rep // SPLIT)] for k in range(SPLIT)]
    share_rows = slot_rows // n_rep
    shares = lax.all_to_all(
        owned.reshape(n_rep // SPLIT, share_rows, head), "rep", 0, 0, axis_index_groups=fellows
    )
    share = summed([shares[q] for q in range(n_rep // SPLIT)])
    total = lax.all_to_all(jnp.broadcast_to(share[None], (n_rep,) + share.shape), "rep", 0, 0)
    weight_grad = finished(total.reshape(slot_rows, head), share_rows)
    return (input_grad, weight_grad)


def solution(mesh):
    placed = (P(("rep", "dp"), None), P(("rep", "dp"), "tp"), P("dp", "tp"), P(), P(("rep", "dp")))
    return jax.shard_map(
        on_device,
        mesh=mesh,
        in_specs=placed,
        out_specs=(P(("rep", "dp"), "tp"), P("dp", "tp")),
        check_vma=False,
    )
```

```python
import functools

import jax
import jax.numpy as jnp
from jax import lax
from jax.experimental import pallas as pl
from jax.experimental.pallas import tpu as pltpu
from jax.sharding import PartitionSpec as P

BLOCK = 128
SPLIT = 3
SMALL = pltpu.CompilerParams(vmem_limit_bytes=12 * 1024 * 1024)


def fill_places(blocks_ref, place, slot_blocks, code):
    first = 0
    for owner in range(blocks_ref.shape[0]):
        for at in range(slot_blocks):
            place[first + at] = code(owner, at)
        first = first + blocks_ref[owner]


def grad_kernel(
    chunk, slot_blocks, counts_ref, blocks_ref, hidden_ref, grad_ref, send_ref, keep_ref, place, masked_t, chunks, sems
):
    steps = hidden_ref.shape[1] // chunk

    def load(step):
        return pltpu.make_async_copy(
            hidden_ref.at[:, pl.ds(step * chunk, chunk)], chunks.at[step], sems.at[step]
        )

    for step in range(steps):
        load(step).start()
    core = lax.rem(lax.axis_index("dp"), 2)
    turn = lax.rem(lax.axis_index("rep"), SPLIT)
    half = send_ref.shape[0]
    part_blocks = slot_blocks // SPLIT
    part_first = [lax.rem(part + SPLIT - turn, SPLIT) * (half // SPLIT) for part in range(SPLIT)]
    side = [jnp.where(core == parity, 0, half) for parity in range(2)]

    def code(owner, at):
        row = ((owner // 2) * part_blocks + at % part_blocks) * BLOCK
        return part_first[at // part_blocks] + side[owner % 2] + row

    fill_places(blocks_ref, place, slot_blocks, code)
    send_ref[...] = jnp.zeros_like(send_ref)
    keep_ref[...] = jnp.zeros_like(keep_ref)
    live = lax.broadcasted_iota(jnp.int32, grad_ref.shape, 0) < counts_ref[0]
    masked = jnp.where(live, grad_ref[...].astype(jnp.float32), 0.0)
    masked_t[...] = masked.T.astype(masked_t.dtype)

    def one(step, carry):
        load(step).wait()
        product = jnp.dot(masked_t[...], chunks[step], preferred_element_type=jnp.float32)
        for at in range(chunk // BLOCK):
            row = place[step * (chunk // BLOCK) + at]
            tile = product[:, at * BLOCK:(at + 1) * BLOCK].astype(send_ref.dtype)

            @pl.when(row < half)
            def _():
                keep_ref[pl.ds(pl.multiple_of(row, BLOCK), BLOCK), :] = tile

            @pl.when(row >= half)
            def _():
                send_ref[pl.ds(pl.multiple_of(row - half, BLOCK), BLOCK), :] = tile

        return carry

    lax.fori_loop(0, steps, one, 0)


def grad_products(counts, shard_blocks, hidden, grad, slot_rows):
    rows, width = hidden.shape
    owners = shard_blocks.shape[0]
    chunk = 1024
    steps = width // chunk
    half = (owners // 2) * slot_rows
    slot_blocks = slot_rows // BLOCK
    out = jax.ShapeDtypeStruct((half, grad.shape[1]), jnp.bfloat16)
    vmem = pl.BlockSpec(memory_space=pltpu.VMEM)
    return pl.pallas_call(
        functools.partial(grad_kernel, chunk, slot_blocks),
        in_specs=[
            pl.BlockSpec(memory_space=pltpu.SMEM),
            pl.BlockSpec(memory_space=pltpu.SMEM),
            pl.BlockSpec(memory_space=pltpu.HBM),
            vmem,
        ],
        out_specs=[vmem, vmem],
        out_shape=[out, out],
        scratch_shapes=[
            pltpu.SMEM((width // BLOCK + slot_blocks,), jnp.int32),
            pltpu.VMEM((grad.shape[1], rows), jnp.bfloat16),
            pltpu.VMEM((steps, rows, chunk), jnp.bfloat16),
            pltpu.SemaphoreType.DMA((steps,)),
        ],
        compiler_params=pltpu.CompilerParams(vmem_limit_bytes=59 * 1024 * 1024),
        cost_estimate=pl.CostEstimate(
            flops=2 * rows * width * grad.shape[1], bytes_accessed=2 * rows * width + 4 * half * 128, transcendentals=0
        ),
        name="grad_products",
    )(counts, shard_blocks, hidden, grad)


def pair_kernel(keep_ref, received_ref, *outs):
    rows = outs[0].shape[0]
    for k, out in enumerate(outs):
        here = pl.ds(k * rows, rows)
        total = keep_ref[here, :].astype(jnp.float32) + received_ref[here, :].astype(jnp.float32)
        out[...] = total.astype(out.dtype)


def paired_parts(keep, received):
    out = jax.ShapeDtypeStruct((keep.shape[0] // SPLIT, keep.shape[1]), keep.dtype)
    return pl.pallas_call(pair_kernel, out_shape=[out] * SPLIT, compiler_params=SMALL, name="pair_parts")(keep, received)


def summed(parts):
    total = parts[0].astype(jnp.float32)
    for part in parts[1:]:
        total = total + part.astype(jnp.float32)
    return total.astype(parts[0].dtype)


def finish_kernel(share, total_ref, out_ref):
    n_rep = total_ref.shape[0] // share
    per = out_ref.shape[0] // SPLIT
    rows = [None] * (out_ref.shape[0] // share)
    for rep in range(n_rep):
        first = (rep % SPLIT) * per + (rep // SPLIT) * share
        rows[first // share] = total_ref[rep * share:(rep + 1) * share, :].astype(out_ref.dtype)
    slot = jnp.concatenate(rows, axis=0)
    for at in range(out_ref.shape[0] // BLOCK):
        out_ref[at * BLOCK:(at + 1) * BLOCK, :] = slot[at * BLOCK:(at + 1) * BLOCK, :].T


def finished(total, share):
    return pl.pallas_call(
        functools.partial(finish_kernel, share),
        out_shape=jax.ShapeDtypeStruct(total.shape, jnp.float32),
        compiler_params=SMALL,
        name="finish_weight_grad",
    )(total)


def compact_kernel(slot_blocks, n_tp, blocks_ref, mine_ref, other_ref, grad_ref, *rest):
    outs, place = rest[:n_tp], rest[n_tp]
    core = lax.rem(lax.axis_index("dp"), 2)
    index = lax.axis_index("tp")
    half = mine_ref.shape[0]
    side = [jnp.where(core == parity, 0, half) for parity in range(2)]
    fill_places(
        blocks_ref, place, slot_blocks,
        lambda owner, at: side[owner % 2] + ((owner // 2) * slot_blocks + at) * BLOCK,
    )
    per = (outs[0].shape[0] - grad_ref.shape[0]) // BLOCK
    for k, out_ref in enumerate(outs):
        first = lax.rem(index + k, n_tp) * per
        for at in range(per):
            source = place[first + at]

            @pl.when(source < half)
            def _():
                out_ref[at * BLOCK:(at + 1) * BLOCK, :] = mine_ref[pl.ds(pl.multiple_of(source, BLOCK), BLOCK), :]

            @pl.when(source >= half)
            def _():
                out_ref[at * BLOCK:(at + 1) * BLOCK, :] = other_ref[
                    pl.ds(pl.multiple_of(source - half, BLOCK), BLOCK), :
                ]

        out_ref[per * BLOCK:, :] = grad_ref[...]


def compacted(shard_blocks, mine, other, grad, slot_rows, n_tp, width):
    slot_blocks = slot_rows // BLOCK
    rows = width // n_tp + grad.shape[0]
    vmem = pl.BlockSpec(memory_space=pltpu.VMEM)
    return pl.pallas_call(
        functools.partial(compact_kernel, slot_blocks, n_tp),
        in_specs=[pl.BlockSpec(memory_space=pltpu.SMEM), vmem, vmem, vmem],
        out_specs=[vmem] * n_tp,
        out_shape=[jax.ShapeDtypeStruct((rows, grad.shape[1]), grad.dtype)] * n_tp,
        scratch_shapes=[pltpu.SMEM((width // BLOCK + slot_blocks,), jnp.int32)],
        compiler_params=SMALL,
        cost_estimate=pl.CostEstimate(flops=0, bytes_accessed=4 * width * grad.shape[1], transcendentals=0),
        name="compact_rows",
    )(shard_blocks, mine, other, grad)


def input_kernel(heads, counts_ref, *refs):
    weights, grads = refs[:heads], refs[heads:2 * heads]
    out_ref, masked = refs[2 * heads:]

    @pl.when(pl.program_id(0) == 0)
    def _():
        for h in range(heads):
            grad = grads[h][...].astype(jnp.float32)
            live = lax.broadcasted_iota(jnp.int32, grad.shape, 0) < counts_ref[0]
            masked[:, h * BLOCK:(h + 1) * BLOCK] = jnp.where(live, grad, 0.0).astype(masked.dtype)

    weight = jnp.concatenate([w[...] for w in weights], axis=1)
    out_ref[...] = lax.dot_general(
        masked[...], weight, (((1,), (1,)), ((), ())), preferred_element_type=jnp.float32
    ).astype(out_ref.dtype)


def input_product(counts, parts, rows_dev):
    n = len(parts)
    rows, head = parts[0].shape[0] - rows_dev, parts[0].shape[1]
    chunk = 512
    return pl.pallas_call(
        functools.partial(input_kernel, n),
        grid=(rows // chunk,),
        in_specs=[pl.BlockSpec(memory_space=pltpu.SMEM)]
        + [pl.BlockSpec((chunk, head), lambda i: (i, 0))] * n
        + [pl.BlockSpec((pl.Element(rows_dev), pl.Element(head)), lambda i: (rows, 0))] * n,
        out_specs=pl.BlockSpec((rows_dev, chunk), lambda i: (0, i)),
        out_shape=jax.ShapeDtypeStruct((rows_dev, rows), jnp.bfloat16),
        scratch_shapes=[pltpu.VMEM((rows_dev, head * n), jnp.bfloat16)],
        compiler_params=pltpu.CompilerParams(vmem_limit_bytes=16 * 1024 * 1024),
        cost_estimate=pl.CostEstimate(
            flops=2 * rows_dev * rows * head * n, bytes_accessed=2 * rows * (head * n + rows_dev), transcendentals=0
        ),
        name="input_grad",
    )(counts, *parts, *parts)


def ordered(array, other):
    return lax.optimization_barrier((array, other))[0]


def on_device(hidden_in, value_grad, weight_shards, shard_blocks, token_counts):
    rows_dev, width = hidden_in.shape
    slot_rows, head = weight_shards.shape
    n_dp, n_tp, n_rep = lax.axis_size("dp"), lax.axis_size("tp"), lax.axis_size("rep")
    n_y = n_dp // 2
    core_swap = [(i, i ^ 1) for i in range(n_dp)]
    along_y = [[c + 2 * y for y in range(n_y)] for c in range(2)]
    up = [(i, (i + 1) % n_rep) for i in range(n_rep)]
    down = [(i, (i - 1) % n_rep) for i in range(n_rep)]

    held = lax.all_to_all(
        jnp.broadcast_to(weight_shards[None], (n_y,) + weight_shards.shape), "dp", 0, 0, axis_index_groups=along_y
    ).reshape(n_y * slot_rows, head)
    send, keep = grad_products(token_counts, shard_blocks, hidden_in, value_grad, slot_rows)
    received = lax.ppermute(send, "dp", core_swap)
    stay, to_next, to_last = paired_parts(keep, received)

    other = lax.ppermute(held, "dp", core_swap)
    sent = compacted(shard_blocks, held, other, value_grad, slot_rows, n_tp, width)
    parts = [sent[0]] + [
        lax.ppermute(sent[k], "tp", [(i, (i + k) % n_tp) for i in range(n_tp)]) for k in range(1, n_tp)
    ]
    input_grad = input_product(token_counts, parts, rows_dev)

    part = summed([stay, lax.ppermute(to_next, "rep", up), lax.ppermute(to_last, "rep", down)])
    spread = lax.all_to_all(part.reshape(n_y, slot_rows // SPLIT, head), "dp", 0, 0, axis_index_groups=along_y)
    spread = ordered(spread, sent[0])
    owned = summed([spread[y] for y in range(n_y)])
    fellows = [[k + SPLIT * q for q in range(n_rep // SPLIT)] for k in range(SPLIT)]
    share_rows = slot_rows // n_rep
    shares = lax.all_to_all(
        owned.reshape(n_rep // SPLIT, share_rows, head), "rep", 0, 0, axis_index_groups=fellows
    )
    share = summed([shares[q] for q in range(n_rep // SPLIT)])
    total = lax.all_to_all(jnp.broadcast_to(share[None], (n_rep,) + share.shape), "rep", 0, 0)
    weight_grad = finished(total.reshape(slot_rows, head), share_rows)
    return (input_grad, weight_grad)


def solution(mesh):
    placed = (P(("rep", "dp"), None), P(("rep", "dp"), "tp"), P("dp", "tp"), P(), P(("rep", "dp")))
    return jax.shard_map(
        on_device,
        mesh=mesh,
        in_specs=placed,
        out_specs=(P(("rep", "dp"), "tp"), P("dp", "tp")),
        check_vma=False,
    )
```

```python
import functools

import jax
import jax.numpy as jnp
from jax import lax
from jax.experimental import pallas as pl
from jax.experimental.pallas import tpu as pltpu
from jax.sharding import PartitionSpec as P

BLOCK = 128
SPLIT = 3
PIECE = 32
SMALL = pltpu.CompilerParams(vmem_limit_bytes=12 * 1024 * 1024)


def fill_places(blocks_ref, place, slot_blocks, code):
    first = 0
    for owner in range(blocks_ref.shape[0]):
        for at in range(slot_blocks):
            place[first + at] = code(owner, at)
        first = first + blocks_ref[owner]


def grad_kernel(
    chunk, slot_blocks, counts_ref, blocks_ref, hidden_ref, grad_ref, send_ref, keep_ref, place, masked_t, chunks, sems
):
    steps = hidden_ref.shape[1] // chunk

    def load(step):
        return pltpu.make_async_copy(
            hidden_ref.at[:, pl.ds(step * chunk, chunk)], chunks.at[step], sems.at[step]
        )

    for step in range(steps):
        load(step).start()
    core = lax.rem(lax.axis_index("dp"), 2)
    turn = lax.rem(lax.axis_index("rep"), SPLIT)
    half = send_ref.shape[0]
    part_blocks = slot_blocks // SPLIT
    part_first = [lax.rem(part + SPLIT - turn, SPLIT) * (half // SPLIT) for part in range(SPLIT)]
    side = [jnp.where(core == parity, 0, half) for parity in range(2)]

    def code(owner, at):
        row = ((owner // 2) * part_blocks + at % part_blocks) * BLOCK
        return part_first[at // part_blocks] + side[owner % 2] + row

    fill_places(blocks_ref, place, slot_blocks, code)
    send_ref[...] = jnp.zeros_like(send_ref)
    keep_ref[...] = jnp.zeros_like(keep_ref)
    live = lax.broadcasted_iota(jnp.int32, grad_ref.shape, 0) < counts_ref[0]
    masked = jnp.where(live, grad_ref[...].astype(jnp.float32), 0.0)
    masked_t[...] = masked.T.astype(masked_t.dtype)

    def one(step, carry):
        load(step).wait()
        product = jnp.dot(masked_t[...], chunks[step], preferred_element_type=jnp.float32)
        for at in range(chunk // BLOCK):
            row = place[step * (chunk // BLOCK) + at]
            tile = product[:, at * BLOCK:(at + 1) * BLOCK].astype(send_ref.dtype)

            @pl.when(row < half)
            def _():
                keep_ref[pl.ds(pl.multiple_of(row, BLOCK), BLOCK), :] = tile

            @pl.when(row >= half)
            def _():
                send_ref[pl.ds(pl.multiple_of(row - half, BLOCK), BLOCK), :] = tile

        return carry

    lax.fori_loop(0, steps, one, 0)


def grad_products(counts, shard_blocks, hidden, grad, slot_rows):
    rows, width = hidden.shape
    owners = shard_blocks.shape[0]
    chunk = 1024
    steps = width // chunk
    half = (owners // 2) * slot_rows
    slot_blocks = slot_rows // BLOCK
    out = jax.ShapeDtypeStruct((half, grad.shape[1]), jnp.bfloat16)
    vmem = pl.BlockSpec(memory_space=pltpu.VMEM)
    return pl.pallas_call(
        functools.partial(grad_kernel, chunk, slot_blocks),
        in_specs=[
            pl.BlockSpec(memory_space=pltpu.SMEM),
            pl.BlockSpec(memory_space=pltpu.SMEM),
            pl.BlockSpec(memory_space=pltpu.HBM),
            vmem,
        ],
        out_specs=[vmem, vmem],
        out_shape=[out, out],
        scratch_shapes=[
            pltpu.SMEM((width // BLOCK + slot_blocks,), jnp.int32),
            pltpu.VMEM((grad.shape[1], rows), jnp.bfloat16),
            pltpu.VMEM((steps, rows, chunk), jnp.bfloat16),
            pltpu.SemaphoreType.DMA((steps,)),
        ],
        compiler_params=pltpu.CompilerParams(vmem_limit_bytes=59 * 1024 * 1024),
        cost_estimate=pl.CostEstimate(
            flops=2 * rows * width * grad.shape[1], bytes_accessed=2 * rows * width + 4 * half * 128, transcendentals=0
        ),
        name="grad_products",
    )(counts, shard_blocks, hidden, grad)


def pair_kernel(keep_ref, received_ref, *outs):
    rows = outs[0].shape[0]
    for k, out in enumerate(outs):
        here = pl.ds(k * rows, rows)
        total = keep_ref[here, :].astype(jnp.float32) + received_ref[here, :].astype(jnp.float32)
        out[...] = total.astype(out.dtype)


def paired_parts(keep, received):
    out = jax.ShapeDtypeStruct((keep.shape[0] // SPLIT, keep.shape[1]), keep.dtype)
    return pl.pallas_call(pair_kernel, out_shape=[out] * SPLIT, compiler_params=SMALL, name="pair_parts")(keep, received)


def summed(parts):
    total = parts[0].astype(jnp.float32)
    for part in parts[1:]:
        total = total + part.astype(jnp.float32)
    return total.astype(parts[0].dtype)


def finish_kernel(share, total_ref, out_ref):
    n_rep = total_ref.shape[0] // share
    per = out_ref.shape[0] // SPLIT
    rows = [None] * (out_ref.shape[0] // share)
    for rep in range(n_rep):
        first = (rep % SPLIT) * per + (rep // SPLIT) * share
        rows[first // share] = total_ref[rep * share:(rep + 1) * share, :].astype(out_ref.dtype)
    slot = jnp.concatenate(rows, axis=0)
    for at in range(out_ref.shape[0] // BLOCK):
        out_ref[at * BLOCK:(at + 1) * BLOCK, :] = slot[at * BLOCK:(at + 1) * BLOCK, :].T


def finished(total, share):
    return pl.pallas_call(
        functools.partial(finish_kernel, share),
        out_shape=jax.ShapeDtypeStruct(total.shape, jnp.float32),
        compiler_params=SMALL,
        name="finish_weight_grad",
    )(total)


def compact_kernel(slot_blocks, n_tp, blocks_ref, held_ref, grad_ref, *rest):
    outs, place = rest[:n_tp], rest[n_tp]
    core = lax.rem(lax.axis_index("dp"), 2)
    index = lax.axis_index("tp")
    side = [jnp.where(core == parity, 0, slot_blocks) for parity in range(2)]
    fill_places(
        blocks_ref, place, slot_blocks,
        lambda owner, at: (side[owner % 2] + (owner // 2) * 2 * slot_blocks + at) * PIECE,
    )
    per = (outs[0].shape[0] - grad_ref.shape[0]) // PIECE
    for k, out_ref in enumerate(outs):
        first = lax.rem(index + k, n_tp) * per
        for at in range(per):
            source = pl.multiple_of(place[first + at], PIECE)
            out_ref[at * PIECE:(at + 1) * PIECE, :] = held_ref[pl.ds(source, PIECE), :]
        out_ref[per * PIECE:, :] = grad_ref[...]


def compacted(shard_blocks, held, grad, slot_rows, n_tp, width):
    n_blocks = width // BLOCK
    slot_blocks = slot_rows // BLOCK
    rows = n_blocks // n_tp * PIECE + grad.shape[0]
    vmem = pl.BlockSpec(memory_space=pltpu.VMEM)
    return pl.pallas_call(
        functools.partial(compact_kernel, slot_blocks, n_tp),
        in_specs=[pl.BlockSpec(memory_space=pltpu.SMEM), vmem, vmem],
        out_specs=[vmem] * n_tp,
        out_shape=[jax.ShapeDtypeStruct((rows, grad.shape[1]), grad.dtype)] * n_tp,
        scratch_shapes=[pltpu.SMEM((n_blocks + slot_blocks,), jnp.int32)],
        compiler_params=SMALL,
        cost_estimate=pl.CostEstimate(flops=0, bytes_accessed=2 * rows * grad.shape[1], transcendentals=0),
        name="compact_rows",
    )(shard_blocks, held, grad)


def stack_kernel(heads, *refs):
    own, far, out_ref = refs[:heads], refs[heads:heads + 2], refs[-1]
    half = heads // 2
    for h in range(heads):
        out_ref[h] = own[h][: out_ref.shape[1], :]
        out_ref[heads + h] = far[h // half][h % half]


def stacked(own, far, other):
    n = len(own)
    _, pieces, head = far[0].shape
    vmem = pl.BlockSpec(memory_space=pltpu.VMEM)
    return pl.pallas_call(
        functools.partial(stack_kernel, n),
        in_specs=[vmem] * (n + 2) + [pl.BlockSpec(memory_space=pl.ANY)],
        out_specs=vmem,
        out_shape=jax.ShapeDtypeStruct((2 * n, pieces, head), own[0].dtype),
        compiler_params=SMALL,
        cost_estimate=pl.CostEstimate(flops=0, bytes_accessed=8 * n * pieces * head, transcendentals=0),
        name="stack_rows",
    )(*own, *far, other)


def input_kernel(heads, counts_ref, *refs):
    own, far, other_ref = refs[:heads], refs[heads:heads + 2], refs[heads + 2]
    grads = refs[heads + 3:2 * heads + 3]
    out_ref, masked, weight = refs[2 * heads + 3:]
    turn = lax.rem(lax.axis_index("rep"), 2)
    core = lax.rem(lax.axis_index("dp"), 2)
    blocks = own[0].shape[0] // PIECE
    half = heads // 2

    @pl.when(pl.program_id(0) == 0)
    def _():
        for h in range(heads):
            grad = grads[h][...].astype(jnp.float32)
            live = lax.broadcasted_iota(jnp.int32, grad.shape, 0) < counts_ref[0]
            masked[:, h * BLOCK:(h + 1) * BLOCK] = jnp.where(live, grad, 0.0).astype(masked.dtype)

    for h in range(heads):
        sources = (
            (own[h], turn, core),
            (far[h // half].at[h % half], 1 - turn, core),
            (other_ref.at[h], turn, 1 - core),
            (other_ref.at[heads + h], 1 - turn, 1 - core),
        )
        for ref, its_turn, its_core in sources:
            first = (2 * its_turn + its_core) * PIECE
            for b in range(blocks):
                rows = pl.ds(pl.multiple_of(b * BLOCK + first, PIECE), PIECE)
                weight[rows, h * BLOCK:(h + 1) * BLOCK] = ref[b * PIECE:(b + 1) * PIECE, :]

    out_ref[...] = lax.dot_general(
        masked[...], weight[...], (((1,), (1,)), ((), ())), preferred_element_type=jnp.float32
    ).astype(out_ref.dtype)


def input_product(counts, own, far, other, rows_dev):
    n_tp = len(own)
    _, pieces, head = other.shape
    steps = 4
    blocks = pieces // PIECE // steps
    chunk = blocks * BLOCK
    rows = blocks * PIECE
    return pl.pallas_call(
        functools.partial(input_kernel, n_tp),
        grid=(steps,),
        in_specs=[pl.BlockSpec(memory_space=pltpu.SMEM)]
        + [pl.BlockSpec((rows, head), lambda i: (i, 0))] * n_tp
        + [pl.BlockSpec((n_tp // 2, rows, head), lambda i: (0, i, 0))] * 2
        + [pl.BlockSpec((2 * n_tp, rows, head), lambda i: (0, i, 0))]
        + [pl.BlockSpec((pl.Element(rows_dev), pl.Element(head)), lambda i: (pieces, 0))] * n_tp,
        out_specs=pl.BlockSpec((rows_dev, chunk), lambda i: (0, i)),
        out_shape=jax.ShapeDtypeStruct((rows_dev, steps * chunk), jnp.bfloat16),
        scratch_shapes=[
            pltpu.VMEM((rows_dev, head * n_tp), jnp.bfloat16),
            pltpu.VMEM((chunk, head * n_tp), jnp.bfloat16),
        ],
        compiler_params=pltpu.CompilerParams(vmem_limit_bytes=16 * 1024 * 1024),
        cost_estimate=pl.CostEstimate(
            flops=2 * rows_dev * steps * chunk * head * n_tp,
            bytes_accessed=2 * steps * chunk * (head * n_tp + rows_dev),
            transcendentals=0,
        ),
        name="input_grad",
    )(counts, *own, *far, other, *own)


def ordered(array, other):
    return lax.optimization_barrier((array, other))[0]


def on_device(hidden_in, value_grad, weight_shards, shard_blocks, token_counts):
    rows_dev, width = hidden_in.shape
    slot_rows, head = weight_shards.shape
    n_dp, n_tp, n_rep = lax.axis_size("dp"), lax.axis_size("tp"), lax.axis_size("rep")
    n_y = n_dp // 2
    slot_blocks = slot_rows // BLOCK
    core_swap = [(i, i ^ 1) for i in range(n_dp)]
    along_y = [[c + 2 * y for y in range(n_y)] for c in range(2)]
    up = [(i, (i + 1) % n_rep) for i in range(n_rep)]
    down = [(i, (i - 1) % n_rep) for i in range(n_rep)]

    core = lax.rem(lax.axis_index("dp"), 2)
    turn = lax.rem(lax.axis_index("rep"), 2)
    slot = weight_shards.reshape(slot_blocks, BLOCK, head)

    def quarter(of_core):
        rows = lax.dynamic_slice_in_dim(slot, (2 * turn + of_core) * PIECE, PIECE, 1)
        return rows.reshape(slot_blocks * PIECE, head)

    both = jnp.concatenate([quarter(core), lax.ppermute(quarter(1 - core), "dp", core_swap)])
    held = lax.all_to_all(
        jnp.broadcast_to(both[None], (n_y,) + both.shape), "dp", 0, 0, axis_index_groups=along_y
    ).reshape(n_y * both.shape[0], head)
    send, keep = grad_products(token_counts, shard_blocks, hidden_in, value_grad, slot_rows)
    received = lax.ppermute(send, "dp", core_swap)
    stay, to_next, to_last = paired_parts(keep, received)

    part = summed([stay, lax.ppermute(to_next, "rep", up), lax.ppermute(to_last, "rep", down)])
    held = ordered(held, part)
    sent = compacted(shard_blocks, held, value_grad, slot_rows, n_tp, width)
    own = [sent[0]] + [
        lax.ppermute(sent[k], "tp", [(i, (i + k) % n_tp) for i in range(n_tp)]) for k in range(1, n_tp)
    ]
    pieces = [part[: part.shape[0] - rows_dev] for part in own]
    far = [
        lax.ppermute(jnp.stack(pieces[: n_tp // 2]), "rep", up),
        lax.ppermute(jnp.stack(pieces[n_tp // 2:]), "rep", down),
    ]

    spread = lax.all_to_all(part.reshape(n_y, slot_rows // SPLIT, head), "dp", 0, 0, axis_index_groups=along_y)
    spread = ordered(spread, pieces)
    owned = summed([spread[y] for y in range(n_y)])
    fellows = [[k + SPLIT * q for q in range(n_rep // SPLIT)] for k in range(SPLIT)]
    share_rows = slot_rows // n_rep
    shares = lax.all_to_all(
        owned.reshape(n_rep // SPLIT, share_rows, head), "rep", 0, 0, axis_index_groups=fellows
    )
    share = summed([shares[q] for q in range(n_rep // SPLIT)])
    other = lax.ppermute(stacked(own, far, share), "dp", core_swap)
    input_grad = input_product(token_counts, own, far, other, rows_dev)
    total = lax.all_to_all(jnp.broadcast_to(share[None], (n_rep,) + share.shape), "rep", 0, 0)
    weight_grad = finished(total.reshape(slot_rows, head), share_rows)
    return (input_grad, weight_grad)


def solution(mesh):
    placed = (P(("rep", "dp"), None), P(("rep", "dp"), "tp"), P("dp", "tp"), P(), P(("rep", "dp")))
    return jax.shard_map(
        on_device,
        mesh=mesh,
        in_specs=placed,
        out_specs=(P(("rep", "dp"), "tp"), P("dp", "tp")),
        check_vma=False,
    )
```

```python
import functools

import jax
import jax.numpy as jnp
from jax import lax
from jax.experimental import pallas as pl
from jax.experimental.pallas import tpu as pltpu
from jax.sharding import PartitionSpec as P

BLOCK = 128
SPLIT = 3
PIECE = 32
SMALL = pltpu.CompilerParams(vmem_limit_bytes=12 * 1024 * 1024)


def fill_places(blocks_ref, place, slot_blocks, code):
    first = 0
    for owner in range(blocks_ref.shape[0]):
        for at in range(slot_blocks):
            place[first + at] = code(owner, at)
        first = first + blocks_ref[owner]


def grad_kernel(
    chunk, slot_blocks, counts_ref, blocks_ref, hidden_ref, grad_ref, send_ref, keep_ref, place, masked_t, chunks, sems
):
    steps = hidden_ref.shape[1] // chunk

    def load(step):
        return pltpu.make_async_copy(
            hidden_ref.at[:, pl.ds(step * chunk, chunk)], chunks.at[step], sems.at[step]
        )

    for step in range(steps):
        load(step).start()
    core = lax.rem(lax.axis_index("dp"), 2)
    turn = lax.rem(lax.axis_index("rep"), SPLIT)
    half = send_ref.shape[0]
    part_blocks = slot_blocks // SPLIT
    part_first = [lax.rem(part + SPLIT - turn, SPLIT) * (half // SPLIT) for part in range(SPLIT)]
    side = [jnp.where(core == parity, 0, half) for parity in range(2)]

    def code(owner, at):
        row = ((owner // 2) * part_blocks + at % part_blocks) * BLOCK
        return part_first[at // part_blocks] + side[owner % 2] + row

    fill_places(blocks_ref, place, slot_blocks, code)
    send_ref[...] = jnp.zeros_like(send_ref)
    keep_ref[...] = jnp.zeros_like(keep_ref)
    live = lax.broadcasted_iota(jnp.int32, grad_ref.shape, 0) < counts_ref[0]
    masked = jnp.where(live, grad_ref[...].astype(jnp.float32), 0.0)
    masked_t[...] = masked.T.astype(masked_t.dtype)

    def one(step, carry):
        load(step).wait()
        product = jnp.dot(masked_t[...], chunks[step], preferred_element_type=jnp.float32)
        for at in range(chunk // BLOCK):
            row = place[step * (chunk // BLOCK) + at]
            tile = product[:, at * BLOCK:(at + 1) * BLOCK].astype(send_ref.dtype)

            @pl.when(row < half)
            def _():
                keep_ref[pl.ds(pl.multiple_of(row, BLOCK), BLOCK), :] = tile

            @pl.when(row >= half)
            def _():
                send_ref[pl.ds(pl.multiple_of(row - half, BLOCK), BLOCK), :] = tile

        return carry

    lax.fori_loop(0, steps, one, 0)


def grad_products(counts, shard_blocks, hidden, grad, slot_rows):
    rows, width = hidden.shape
    owners = shard_blocks.shape[0]
    chunk = 1024
    steps = width // chunk
    half = (owners // 2) * slot_rows
    slot_blocks = slot_rows // BLOCK
    out = jax.ShapeDtypeStruct((half, grad.shape[1]), jnp.bfloat16)
    vmem = pl.BlockSpec(memory_space=pltpu.VMEM)
    return pl.pallas_call(
        functools.partial(grad_kernel, chunk, slot_blocks),
        in_specs=[
            pl.BlockSpec(memory_space=pltpu.SMEM),
            pl.BlockSpec(memory_space=pltpu.SMEM),
            pl.BlockSpec(memory_space=pltpu.HBM),
            vmem,
        ],
        out_specs=[vmem, vmem],
        out_shape=[out, out],
        scratch_shapes=[
            pltpu.SMEM((width // BLOCK + slot_blocks,), jnp.int32),
            pltpu.VMEM((grad.shape[1], rows), jnp.bfloat16),
            pltpu.VMEM((steps, rows, chunk), jnp.bfloat16),
            pltpu.SemaphoreType.DMA((steps,)),
        ],
        compiler_params=pltpu.CompilerParams(vmem_limit_bytes=59 * 1024 * 1024),
        cost_estimate=pl.CostEstimate(
            flops=2 * rows * width * grad.shape[1], bytes_accessed=2 * rows * width + 4 * half * 128, transcendentals=0
        ),
        name="grad_products",
    )(counts, shard_blocks, hidden, grad)


def pair_kernel(keep_ref, received_ref, *outs):
    rows = outs[0].shape[0]
    for k, out in enumerate(outs):
        here = pl.ds(k * rows, rows)
        total = keep_ref[here, :].astype(jnp.float32) + received_ref[here, :].astype(jnp.float32)
        out[...] = total.astype(out.dtype)


def paired_parts(keep, received):
    out = jax.ShapeDtypeStruct((keep.shape[0] // SPLIT, keep.shape[1]), keep.dtype)
    return pl.pallas_call(pair_kernel, out_shape=[out] * SPLIT, compiler_params=SMALL, name="pair_parts")(keep, received)


def summed(parts):
    total = parts[0].astype(jnp.float32)
    for part in parts[1:]:
        total = total + part.astype(jnp.float32)
    return total.astype(parts[0].dtype)


def finish_kernel(share, total_ref, done_ref, out_ref):
    n_rep = total_ref.shape[0] // share
    per = out_ref.shape[0] // SPLIT
    rows = [None] * (out_ref.shape[0] // share)
    for rep in range(n_rep):
        first = (rep % SPLIT) * per + (rep // SPLIT) * share
        rows[first // share] = total_ref[rep * share:(rep + 1) * share, :].astype(out_ref.dtype)
    slot = jnp.concatenate(rows, axis=0)
    for at in range(out_ref.shape[0] // BLOCK):
        out_ref[at * BLOCK:(at + 1) * BLOCK, :] = slot[at * BLOCK:(at + 1) * BLOCK, :].T


def finished(total, share, done):
    return pl.pallas_call(
        functools.partial(finish_kernel, share),
        in_specs=[pl.BlockSpec(memory_space=pltpu.VMEM), pl.BlockSpec(memory_space=pl.ANY)],
        out_shape=jax.ShapeDtypeStruct(total.shape, jnp.float32),
        compiler_params=SMALL,
        name="finish_weight_grad",
    )(total, done)


def compact_kernel(slot_blocks, n_tp, blocks_ref, held_ref, grad_ref, *rest):
    outs, place = rest[:n_tp], rest[n_tp]
    index = lax.axis_index("tp")
    fill_places(blocks_ref, place, slot_blocks, lambda owner, at: (owner * slot_blocks + at) * PIECE)
    per = (outs[0].shape[0] - grad_ref.shape[0]) // PIECE
    for k, out_ref in enumerate(outs):
        first = lax.rem(index + k, n_tp) * per
        for at in range(per):
            source = pl.multiple_of(place[first + at], PIECE)
            out_ref[at * PIECE:(at + 1) * PIECE, :] = held_ref[pl.ds(source, PIECE), :]
        out_ref[per * PIECE:, :] = grad_ref[...]


def compacted(shard_blocks, held, grad, slot_rows, n_tp, width):
    n_blocks = width // BLOCK
    slot_blocks = slot_rows // BLOCK
    rows = n_blocks // n_tp * PIECE + grad.shape[0]
    vmem = pl.BlockSpec(memory_space=pltpu.VMEM)
    return pl.pallas_call(
        functools.partial(compact_kernel, slot_blocks, n_tp),
        in_specs=[pl.BlockSpec(memory_space=pltpu.SMEM), vmem, vmem],
        out_specs=[vmem] * n_tp,
        out_shape=[jax.ShapeDtypeStruct((rows, grad.shape[1]), grad.dtype)] * n_tp,
        scratch_shapes=[pltpu.SMEM((n_blocks + slot_blocks,), jnp.int32)],
        compiler_params=SMALL,
        cost_estimate=pl.CostEstimate(flops=0, bytes_accessed=2 * rows * grad.shape[1], transcendentals=0),
        name="compact_rows",
    )(shard_blocks, held, grad)


def stack_kernel(heads, *refs):
    own, out_ref = refs[:heads], refs[-1]
    for h in range(heads):
        out_ref[h] = own[h][: out_ref.shape[1], :]


def stacked(own, pieces, done):
    n, head = len(own), own[0].shape[1]
    vmem = pl.BlockSpec(memory_space=pltpu.VMEM)
    return pl.pallas_call(
        functools.partial(stack_kernel, n),
        in_specs=[vmem] * n + [pl.BlockSpec(memory_space=pl.ANY)],
        out_specs=vmem,
        out_shape=jax.ShapeDtypeStruct((n, pieces, head), own[0].dtype),
        compiler_params=SMALL,
        cost_estimate=pl.CostEstimate(flops=0, bytes_accessed=4 * n * pieces * head, transcendentals=0),
        name="stack_rows",
    )(*own, done)


def halve_kernel(own_ref, other_ref, *outs):
    half = own_ref.shape[0] // 2
    for k, out_ref in enumerate(outs):
        out_ref[:half] = own_ref[k * half:(k + 1) * half]
        out_ref[half:] = other_ref[k * half:(k + 1) * half]


def halved(own, other):
    vmem = pl.BlockSpec(memory_space=pltpu.VMEM)
    return pl.pallas_call(
        halve_kernel,
        in_specs=[vmem] * 2,
        out_specs=[vmem] * 2,
        out_shape=[jax.ShapeDtypeStruct(own.shape, own.dtype)] * 2,
        compiler_params=SMALL,
        cost_estimate=pl.CostEstimate(flops=0, bytes_accessed=8 * own.size, transcendentals=0),
        name="halve_heads",
    )(own, other)


def input_kernel(heads, counts_ref, own_ref, other_ref, *refs):
    far, grads = refs[:2], refs[2:heads + 2]
    out_ref, done_ref, masked, weight = refs[heads + 2:]
    turn = lax.rem(lax.axis_index("rep"), 2)
    core = lax.rem(lax.axis_index("dp"), 2)
    blocks = own_ref.shape[1] // PIECE
    half = heads // 2

    @pl.when(pl.program_id(0) == 0)
    def _():
        done_ref[...] = jnp.zeros_like(done_ref)
        for h in range(heads):
            grad = grads[h][...].astype(jnp.float32)
            live = lax.broadcasted_iota(jnp.int32, grad.shape, 0) < counts_ref[0]
            masked[:, h * BLOCK:(h + 1) * BLOCK] = jnp.where(live, grad, 0.0).astype(masked.dtype)

    for h in range(heads):
        sources = (
            (own_ref.at[h], turn, core),
            (other_ref.at[h], turn, 1 - core),
            (far[h // half].at[h % half], 1 - turn, core),
            (far[h // half].at[half + h % half], 1 - turn, 1 - core),
        )
        for ref, its_turn, its_core in sources:
            first = (2 * its_turn + its_core) * PIECE
            for b in range(blocks):
                rows = pl.ds(pl.multiple_of(b * BLOCK + first, PIECE), PIECE)
                weight[rows, h * BLOCK:(h + 1) * BLOCK] = ref[b * PIECE:(b + 1) * PIECE, :]

    out_ref[...] = lax.dot_general(
        masked[...], weight[...], (((1,), (1,)), ((), ())), preferred_element_type=jnp.float32
    ).astype(out_ref.dtype)


def input_product(counts, parts, own, other, far, rows_dev):
    n_tp, pieces, head = own.shape
    steps = 4
    blocks = pieces // PIECE // steps
    chunk = blocks * BLOCK
    piece = pl.BlockSpec((n_tp, blocks * PIECE, head), lambda i: (0, i, 0))
    return pl.pallas_call(
        functools.partial(input_kernel, n_tp),
        grid=(steps,),
        in_specs=[pl.BlockSpec(memory_space=pltpu.SMEM)]
        + [piece] * 4
        + [pl.BlockSpec((pl.Element(rows_dev), pl.Element(head)), lambda i: (pieces, 0))] * n_tp,
        out_specs=[
            pl.BlockSpec((rows_dev, chunk), lambda i: (0, i)),
            pl.BlockSpec((8, 128), lambda i: (0, 0)),
        ],
        out_shape=[
            jax.ShapeDtypeStruct((rows_dev, steps * chunk), jnp.bfloat16),
            jax.ShapeDtypeStruct((8, 128), jnp.float32),
        ],
        scratch_shapes=[
            pltpu.VMEM((rows_dev, head * n_tp), jnp.bfloat16),
            pltpu.VMEM((chunk, head * n_tp), jnp.bfloat16),
        ],
        compiler_params=pltpu.CompilerParams(vmem_limit_bytes=16 * 1024 * 1024),
        cost_estimate=pl.CostEstimate(
            flops=2 * rows_dev * steps * chunk * head * n_tp,
            bytes_accessed=2 * steps * chunk * (head * n_tp + rows_dev),
            transcendentals=0,
        ),
        name="input_grad",
    )(counts, own, other, *far, *parts)


def ordered(array, other):
    return lax.optimization_barrier((array, other))[0]


def on_device(hidden_in, value_grad, weight_shards, shard_blocks, token_counts):
    rows_dev, width = hidden_in.shape
    slot_rows, head = weight_shards.shape
    n_dp, n_tp, n_rep = lax.axis_size("dp"), lax.axis_size("tp"), lax.axis_size("rep")
    n_y = n_dp // 2
    slot_blocks = slot_rows // BLOCK
    core_swap = [(i, i ^ 1) for i in range(n_dp)]
    along_y = [[c + 2 * y for y in range(n_y)] for c in range(2)]
    up = [(i, (i + 1) % n_rep) for i in range(n_rep)]
    down = [(i, (i - 1) % n_rep) for i in range(n_rep)]

    turn = lax.rem(lax.axis_index("rep"), 2)
    halves = lax.dynamic_slice_in_dim(
        weight_shards.reshape(slot_blocks, BLOCK, head), 2 * turn * PIECE, 2 * PIECE, 1
    )
    quarters = halves.reshape(slot_blocks, 2, PIECE, head).swapaxes(0, 1).reshape(1, 2, slot_blocks * PIECE, head)
    held = lax.all_to_all(
        jnp.broadcast_to(quarters, (n_y,) + quarters.shape[1:]).reshape(n_dp, slot_blocks * PIECE, head), "dp", 0, 0
    ).reshape(n_dp * slot_blocks * PIECE, head)
    send, keep = grad_products(token_counts, shard_blocks, hidden_in, value_grad, slot_rows)
    received = lax.ppermute(send, "dp", core_swap)
    stay, to_next, to_last = paired_parts(keep, received)

    part = summed([stay, lax.ppermute(to_next, "rep", up), lax.ppermute(to_last, "rep", down)])
    held = ordered(held, part)
    sent = compacted(shard_blocks, held, value_grad, slot_rows, n_tp, width)
    parts = [sent[0]] + [
        lax.ppermute(sent[k], "tp", [(i, (i + k) % n_tp) for i in range(n_tp)]) for k in range(1, n_tp)
    ]

    spread = lax.all_to_all(part.reshape(n_y, slot_rows // SPLIT, head), "dp", 0, 0, axis_index_groups=along_y)
    owned = summed([spread[y] for y in range(n_y)])
    own = stacked(parts, parts[0].shape[0] - rows_dev, spread)
    other = lax.ppermute(own, "dp", core_swap)
    first, second = halved(own, other)
    far = [lax.ppermute(first, "rep", up), lax.ppermute(second, "rep", down)]
    input_grad, done = input_product(token_counts, parts, own, other, far, rows_dev)

    fellows = [[k + SPLIT * q for q in range(n_rep // SPLIT)] for k in range(SPLIT)]
    share_rows = slot_rows // n_rep
    shares = lax.all_to_all(
        owned.reshape(n_rep // SPLIT, share_rows, head), "rep", 0, 0, axis_index_groups=fellows
    )
    share = summed([shares[q] for q in range(n_rep // SPLIT)])
    total = lax.all_to_all(jnp.broadcast_to(share[None], (n_rep,) + share.shape), "rep", 0, 0)
    weight_grad = finished(total.reshape(slot_rows, head), share_rows, done)
    return (input_grad, weight_grad)


def solution(mesh):
    placed = (P(("rep", "dp"), None), P(("rep", "dp"), "tp"), P("dp", "tp"), P(), P(("rep", "dp")))
    return jax.shard_map(
        on_device,
        mesh=mesh,
        in_specs=placed,
        out_specs=(P(("rep", "dp"), "tp"), P("dp", "tp")),
        check_vma=False,
    )
```

```python
import functools

import jax
import jax.numpy as jnp
from jax import lax
from jax.experimental import pallas as pl
from jax.experimental.pallas import tpu as pltpu
from jax.sharding import PartitionSpec as P

BLOCK = 128
SPLIT = 3
PIECE = 32
SMALL = pltpu.CompilerParams(vmem_limit_bytes=12 * 1024 * 1024)


def fill_places(blocks_ref, place, slot_blocks, code):
    first = 0
    for owner in range(blocks_ref.shape[0]):
        for at in range(slot_blocks):
            place[first + at] = code(owner, at)
        first = first + blocks_ref[owner]


def grad_kernel(
    chunk, slot_blocks, counts_ref, blocks_ref, hidden_ref, grad_ref, send_ref, keep_ref, place, masked_t, chunks, sems
):
    steps = hidden_ref.shape[1] // chunk

    def load(step):
        return pltpu.make_async_copy(
            hidden_ref.at[:, pl.ds(step * chunk, chunk)], chunks.at[step], sems.at[step]
        )

    for step in range(steps):
        load(step).start()
    core = lax.rem(lax.axis_index("dp"), 2)
    turn = lax.rem(lax.axis_index("rep"), SPLIT)
    half = send_ref.shape[0]
    part_blocks = slot_blocks // SPLIT
    part_first = [lax.rem(part + SPLIT - turn, SPLIT) * (half // SPLIT) for part in range(SPLIT)]
    side = [jnp.where(core == parity, 0, half) for parity in range(2)]

    def code(owner, at):
        row = ((owner // 2) * part_blocks + at % part_blocks) * BLOCK
        return part_first[at // part_blocks] + side[owner % 2] + row

    fill_places(blocks_ref, place, slot_blocks, code)
    send_ref[...] = jnp.zeros_like(send_ref)
    keep_ref[...] = jnp.zeros_like(keep_ref)
    live = lax.broadcasted_iota(jnp.int32, grad_ref.shape, 0) < counts_ref[0]
    masked = jnp.where(live, grad_ref[...].astype(jnp.float32), 0.0)
    masked_t[...] = masked.T.astype(masked_t.dtype)

    def one(step, carry):
        load(step).wait()
        product = jnp.dot(masked_t[...], chunks[step], preferred_element_type=jnp.float32)
        for at in range(chunk // BLOCK):
            row = place[step * (chunk // BLOCK) + at]
            tile = product[:, at * BLOCK:(at + 1) * BLOCK].astype(send_ref.dtype)

            @pl.when(row < half)
            def _():
                keep_ref[pl.ds(pl.multiple_of(row, BLOCK), BLOCK), :] = tile

            @pl.when(row >= half)
            def _():
                send_ref[pl.ds(pl.multiple_of(row - half, BLOCK), BLOCK), :] = tile

        return carry

    lax.fori_loop(0, steps, one, 0)


def grad_products(counts, shard_blocks, hidden, grad, slot_rows):
    rows, width = hidden.shape
    owners = shard_blocks.shape[0]
    chunk = 1024
    steps = width // chunk
    half = (owners // 2) * slot_rows
    slot_blocks = slot_rows // BLOCK
    out = jax.ShapeDtypeStruct((half, grad.shape[1]), jnp.bfloat16)
    vmem = pl.BlockSpec(memory_space=pltpu.VMEM)
    return pl.pallas_call(
        functools.partial(grad_kernel, chunk, slot_blocks),
        in_specs=[
            pl.BlockSpec(memory_space=pltpu.SMEM),
            pl.BlockSpec(memory_space=pltpu.SMEM),
            pl.BlockSpec(memory_space=pltpu.HBM),
            vmem,
        ],
        out_specs=[vmem, vmem],
        out_shape=[out, out],
        scratch_shapes=[
            pltpu.SMEM((width // BLOCK + slot_blocks,), jnp.int32),
            pltpu.VMEM((grad.shape[1], rows), jnp.bfloat16),
            pltpu.VMEM((steps, rows, chunk), jnp.bfloat16),
            pltpu.SemaphoreType.DMA((steps,)),
        ],
        compiler_params=pltpu.CompilerParams(vmem_limit_bytes=59 * 1024 * 1024),
        cost_estimate=pl.CostEstimate(
            flops=2 * rows * width * grad.shape[1], bytes_accessed=2 * rows * width + 4 * half * 128, transcendentals=0
        ),
        name="grad_products",
    )(counts, shard_blocks, hidden, grad)


def pair_kernel(keep_ref, received_ref, *outs):
    rows = outs[0].shape[0]
    for k, out in enumerate(outs):
        here = pl.ds(k * rows, rows)
        total = keep_ref[here, :].astype(jnp.float32) + received_ref[here, :].astype(jnp.float32)
        out[...] = total.astype(out.dtype)


def paired_parts(keep, received):
    out = jax.ShapeDtypeStruct((keep.shape[0] // SPLIT, keep.shape[1]), keep.dtype)
    return pl.pallas_call(pair_kernel, out_shape=[out] * SPLIT, compiler_params=SMALL, name="pair_parts")(keep, received)


def summed(parts):
    total = parts[0].astype(jnp.float32)
    for part in parts[1:]:
        total = total + part.astype(jnp.float32)
    return total.astype(parts[0].dtype)


def finish_kernel(own_ref, before_ref, after_ref, done_ref, out_ref):
    turn = lax.rem(lax.axis_index("rep"), SPLIT)
    rows = own_ref.shape[0]
    for shift, ref in ((0, own_ref), (SPLIT - 1, before_ref), (1, after_ref)):
        first = lax.rem(turn + shift, SPLIT) * rows
        for at in range(rows // BLOCK):
            tile = ref[at * BLOCK:(at + 1) * BLOCK, :].astype(out_ref.dtype)
            out_ref[pl.ds(pl.multiple_of(first + at * BLOCK, BLOCK), BLOCK), :] = tile.T


def finished(own, before, after, done):
    return pl.pallas_call(
        finish_kernel,
        in_specs=[pl.BlockSpec(memory_space=pltpu.VMEM)] * 3 + [pl.BlockSpec(memory_space=pl.ANY)],
        out_shape=jax.ShapeDtypeStruct((SPLIT * own.shape[0], own.shape[1]), jnp.float32),
        compiler_params=SMALL,
        name="finish_weight_grad",
    )(own, before, after, done)


def compact_kernel(slot_blocks, n_tp, blocks_ref, held_ref, grad_ref, *rest):
    outs, place = rest[:n_tp], rest[n_tp]
    index = lax.axis_index("tp")
    fill_places(blocks_ref, place, slot_blocks, lambda owner, at: (owner * slot_blocks + at) * PIECE)
    per = (outs[0].shape[0] - grad_ref.shape[0]) // PIECE
    for k, out_ref in enumerate(outs):
        first = lax.rem(index + k, n_tp) * per
        for at in range(per):
            source = pl.multiple_of(place[first + at], PIECE)
            out_ref[at * PIECE:(at + 1) * PIECE, :] = held_ref[pl.ds(source, PIECE), :]
        out_ref[per * PIECE:, :] = grad_ref[...]


def compacted(shard_blocks, held, grad, slot_rows, n_tp, width):
    n_blocks = width // BLOCK
    slot_blocks = slot_rows // BLOCK
    rows = n_blocks // n_tp * PIECE + grad.shape[0]
    vmem = pl.BlockSpec(memory_space=pltpu.VMEM)
    return pl.pallas_call(
        functools.partial(compact_kernel, slot_blocks, n_tp),
        in_specs=[pl.BlockSpec(memory_space=pltpu.SMEM), vmem, vmem],
        out_specs=[vmem] * n_tp,
        out_shape=[jax.ShapeDtypeStruct((rows, grad.shape[1]), grad.dtype)] * n_tp,
        scratch_shapes=[pltpu.SMEM((n_blocks + slot_blocks,), jnp.int32)],
        compiler_params=SMALL,
        cost_estimate=pl.CostEstimate(flops=0, bytes_accessed=2 * rows * grad.shape[1], transcendentals=0),
        name="compact_rows",
    )(shard_blocks, held, grad)


def stack_kernel(heads, *refs):
    own, out_ref = refs[:heads], refs[-1]
    for h in range(heads):
        out_ref[h] = own[h][: out_ref.shape[1], :]


def stacked(own, pieces, done):
    n, head = len(own), own[0].shape[1]
    vmem = pl.BlockSpec(memory_space=pltpu.VMEM)
    return pl.pallas_call(
        functools.partial(stack_kernel, n),
        in_specs=[vmem] * n + [pl.BlockSpec(memory_space=pl.ANY)],
        out_specs=vmem,
        out_shape=jax.ShapeDtypeStruct((n, pieces, head), own[0].dtype),
        compiler_params=SMALL,
        cost_estimate=pl.CostEstimate(flops=0, bytes_accessed=4 * n * pieces * head, transcendentals=0),
        name="stack_rows",
    )(*own, done)


def halve_kernel(own_ref, other_ref, *outs):
    half = own_ref.shape[0] // 2
    for k, out_ref in enumerate(outs):
        out_ref[:half] = own_ref[k * half:(k + 1) * half]
        out_ref[half:] = other_ref[k * half:(k + 1) * half]


def halved(own, other):
    vmem = pl.BlockSpec(memory_space=pltpu.VMEM)
    return pl.pallas_call(
        halve_kernel,
        in_specs=[vmem] * 2,
        out_specs=[vmem] * 2,
        out_shape=[jax.ShapeDtypeStruct(own.shape, own.dtype)] * 2,
        compiler_params=SMALL,
        cost_estimate=pl.CostEstimate(flops=0, bytes_accessed=8 * own.size, transcendentals=0),
        name="halve_heads",
    )(own, other)


def input_kernel(heads, counts_ref, own_ref, other_ref, *refs):
    far, grads = refs[:2], refs[2:heads + 2]
    out_ref, done_ref, masked, weight = refs[heads + 2:]
    turn = lax.rem(lax.axis_index("rep"), 2)
    core = lax.rem(lax.axis_index("dp"), 2)
    blocks = own_ref.shape[1] // PIECE
    half = heads // 2

    @pl.when(pl.program_id(0) == 0)
    def _():
        done_ref[...] = jnp.zeros_like(done_ref)
        for h in range(heads):
            grad = grads[h][...].astype(jnp.float32)
            live = lax.broadcasted_iota(jnp.int32, grad.shape, 0) < counts_ref[0]
            masked[:, h * BLOCK:(h + 1) * BLOCK] = jnp.where(live, grad, 0.0).astype(masked.dtype)

    for h in range(heads):
        sources = (
            (own_ref.at[h], turn, core),
            (other_ref.at[h], turn, 1 - core),
            (far[h // half].at[h % half], 1 - turn, core),
            (far[h // half].at[half + h % half], 1 - turn, 1 - core),
        )
        for ref, its_turn, its_core in sources:
            first = (2 * its_turn + its_core) * PIECE
            for b in range(blocks):
                rows = pl.ds(pl.multiple_of(b * BLOCK + first, PIECE), PIECE)
                weight[rows, h * BLOCK:(h + 1) * BLOCK] = ref[b * PIECE:(b + 1) * PIECE, :]

    out_ref[...] = lax.dot_general(
        masked[...], weight[...], (((1,), (1,)), ((), ())), preferred_element_type=jnp.float32
    ).astype(out_ref.dtype)


def input_product(counts, parts, own, other, far, rows_dev):
    n_tp, pieces, head = own.shape
    steps = 4
    blocks = pieces // PIECE // steps
    chunk = blocks * BLOCK
    piece = pl.BlockSpec((n_tp, blocks * PIECE, head), lambda i: (0, i, 0))
    return pl.pallas_call(
        functools.partial(input_kernel, n_tp),
        grid=(steps,),
        in_specs=[pl.BlockSpec(memory_space=pltpu.SMEM)]
        + [piece] * 4
        + [pl.BlockSpec((pl.Element(rows_dev), pl.Element(head)), lambda i: (pieces, 0))] * n_tp,
        out_specs=[
            pl.BlockSpec((rows_dev, chunk), lambda i: (0, i)),
            pl.BlockSpec((8, 128), lambda i: (0, 0)),
        ],
        out_shape=[
            jax.ShapeDtypeStruct((rows_dev, steps * chunk), jnp.bfloat16),
            jax.ShapeDtypeStruct((8, 128), jnp.float32),
        ],
        scratch_shapes=[
            pltpu.VMEM((rows_dev, head * n_tp), jnp.bfloat16),
            pltpu.VMEM((chunk, head * n_tp), jnp.bfloat16),
        ],
        compiler_params=pltpu.CompilerParams(vmem_limit_bytes=16 * 1024 * 1024),
        cost_estimate=pl.CostEstimate(
            flops=2 * rows_dev * steps * chunk * head * n_tp,
            bytes_accessed=2 * steps * chunk * (head * n_tp + rows_dev),
            transcendentals=0,
        ),
        name="input_grad",
    )(counts, own, other, *far, *parts)


def ordered(array, other):
    return lax.optimization_barrier((array, other))[0]


def on_device(hidden_in, value_grad, weight_shards, shard_blocks, token_counts):
    rows_dev, width = hidden_in.shape
    slot_rows, head = weight_shards.shape
    n_dp, n_tp, n_rep = lax.axis_size("dp"), lax.axis_size("tp"), lax.axis_size("rep")
    n_y = n_dp // 2
    slot_blocks = slot_rows // BLOCK
    core_swap = [(i, i ^ 1) for i in range(n_dp)]
    along_y = [[c + 2 * y for y in range(n_y)] for c in range(2)]
    up = [(i, (i + 1) % n_rep) for i in range(n_rep)]
    down = [(i, (i - 1) % n_rep) for i in range(n_rep)]

    turn = lax.rem(lax.axis_index("rep"), 2)
    halves = lax.dynamic_slice_in_dim(
        weight_shards.reshape(slot_blocks, BLOCK, head), 2 * turn * PIECE, 2 * PIECE, 1
    )
    quarters = halves.reshape(slot_blocks, 2, PIECE, head).swapaxes(0, 1).reshape(1, 2, slot_blocks * PIECE, head)
    held = lax.all_to_all(
        jnp.broadcast_to(quarters, (n_y,) + quarters.shape[1:]).reshape(n_dp, slot_blocks * PIECE, head), "dp", 0, 0
    ).reshape(n_dp * slot_blocks * PIECE, head)
    send, keep = grad_products(token_counts, shard_blocks, hidden_in, value_grad, slot_rows)
    received = lax.ppermute(send, "dp", core_swap)
    stay, to_next, to_last = paired_parts(keep, received)

    part = summed([stay, lax.ppermute(to_next, "rep", up), lax.ppermute(to_last, "rep", down)])
    held = ordered(held, part)
    sent = compacted(shard_blocks, held, value_grad, slot_rows, n_tp, width)
    parts = [sent[0]] + [
        lax.ppermute(sent[k], "tp", [(i, (i + k) % n_tp) for i in range(n_tp)]) for k in range(1, n_tp)
    ]

    spread = lax.all_to_all(part.reshape(n_y, slot_rows // SPLIT, head), "dp", 0, 0, axis_index_groups=along_y)
    owned = summed([spread[y] for y in range(n_y)])
    own = stacked(parts, parts[0].shape[0] - rows_dev, spread)
    other = lax.ppermute(own, "dp", core_swap)
    first, second = halved(own, other)
    far = [lax.ppermute(first, "rep", up), lax.ppermute(second, "rep", down)]
    input_grad, done = input_product(token_counts, parts, own, other, far, rows_dev)

    n_fellows = n_rep // SPLIT
    fellows = [[k + SPLIT * q for q in range(n_fellows)] for k in range(SPLIT)]
    shares = lax.all_to_all(
        jnp.broadcast_to(owned[None], (n_fellows,) + owned.shape), "rep", 0, 0, axis_index_groups=fellows
    )
    third = summed([shares[q] for q in range(n_fellows)])
    weight_grad = finished(third, lax.ppermute(third, "rep", up), lax.ppermute(third, "rep", down), done)
    return (input_grad, weight_grad)


def solution(mesh):
    placed = (P(("rep", "dp"), None), P(("rep", "dp"), "tp"), P("dp", "tp"), P(), P(("rep", "dp")))
    return jax.shard_map(
        on_device,
        mesh=mesh,
        in_specs=placed,
        out_specs=(P(("rep", "dp"), "tp"), P("dp", "tp")),
        check_vma=False,
    )
```

```python
import functools

import jax
import jax.numpy as jnp
from jax import lax
from jax.experimental import pallas as pl
from jax.experimental.pallas import tpu as pltpu
from jax.sharding import PartitionSpec as P

BLOCK = 128
SPLIT = 3
AHEAD = 3
PIECE = 32
SMALL = pltpu.CompilerParams(vmem_limit_bytes=12 * 1024 * 1024)


def fill_places(blocks_ref, place, slot_blocks, code):
    first = 0
    for owner in range(blocks_ref.shape[0]):
        for at in range(slot_blocks):
            place[first + at] = code(owner, at)
        first = first + blocks_ref[owner]


def grad_kernel(
    chunk, slot_blocks, counts_ref, blocks_ref, hidden_ref, grad_ref, send_ref, keep_ref, place, masked_t, chunks, sems
):
    steps = hidden_ref.shape[1] // chunk

    def load(step):
        return pltpu.make_async_copy(
            hidden_ref.at[:, pl.ds(step * chunk, chunk)], chunks.at[step], sems.at[step]
        )

    for step in range(min(AHEAD, steps)):
        load(step).start()
    core = lax.rem(lax.axis_index("dp"), 2)
    turn = lax.rem(lax.axis_index("rep"), SPLIT)
    half = send_ref.shape[0]
    part_blocks = slot_blocks // SPLIT
    part_first = [lax.rem(part + SPLIT - turn, SPLIT) * (half // SPLIT) for part in range(SPLIT)]
    side = [jnp.where(core == parity, 0, half) for parity in range(2)]

    def code(owner, at):
        row = ((owner // 2) * part_blocks + at % part_blocks) * BLOCK
        return part_first[at // part_blocks] + side[owner % 2] + row

    fill_places(blocks_ref, place, slot_blocks, code)
    send_ref[...] = jnp.zeros_like(send_ref)
    keep_ref[...] = jnp.zeros_like(keep_ref)
    live = lax.broadcasted_iota(jnp.int32, grad_ref.shape, 0) < counts_ref[0]
    masked = jnp.where(live, grad_ref[...].astype(jnp.float32), 0.0)
    masked_t[...] = masked.T.astype(masked_t.dtype)

    def one(step, carry):
        load(step).wait()

        @pl.when(step + AHEAD < steps)
        def _():
            load(step + AHEAD).start()

        product = jnp.dot(masked_t[...], chunks[step], preferred_element_type=jnp.float32)
        for at in range(chunk // BLOCK):
            row = place[step * (chunk // BLOCK) + at]
            tile = product[:, at * BLOCK:(at + 1) * BLOCK].astype(send_ref.dtype)

            @pl.when(row < half)
            def _():
                keep_ref[pl.ds(pl.multiple_of(row, BLOCK), BLOCK), :] = tile

            @pl.when(row >= half)
            def _():
                send_ref[pl.ds(pl.multiple_of(row - half, BLOCK), BLOCK), :] = tile

        return carry

    lax.fori_loop(0, steps, one, 0)


def grad_products(counts, shard_blocks, hidden, grad, slot_rows):
    rows, width = hidden.shape
    owners = shard_blocks.shape[0]
    chunk = 1024
    steps = width // chunk
    half = (owners // 2) * slot_rows
    slot_blocks = slot_rows // BLOCK
    out = jax.ShapeDtypeStruct((half, grad.shape[1]), jnp.bfloat16)
    vmem = pl.BlockSpec(memory_space=pltpu.VMEM)
    return pl.pallas_call(
        functools.partial(grad_kernel, chunk, slot_blocks),
        in_specs=[
            pl.BlockSpec(memory_space=pltpu.SMEM),
            pl.BlockSpec(memory_space=pltpu.SMEM),
            pl.BlockSpec(memory_space=pltpu.HBM),
            vmem,
        ],
        out_specs=[vmem, vmem],
        out_shape=[out, out],
        scratch_shapes=[
            pltpu.SMEM((width // BLOCK + slot_blocks,), jnp.int32),
            pltpu.VMEM((grad.shape[1], rows), jnp.bfloat16),
            pltpu.VMEM((steps, rows, chunk), jnp.bfloat16),
            pltpu.SemaphoreType.DMA((steps,)),
        ],
        compiler_params=pltpu.CompilerParams(vmem_limit_bytes=59 * 1024 * 1024),
        cost_estimate=pl.CostEstimate(
            flops=2 * rows * width * grad.shape[1], bytes_accessed=2 * rows * width + 4 * half * 128, transcendentals=0
        ),
        name="grad_products",
    )(counts, shard_blocks, hidden, grad)


def summed(parts):
    total = parts[0].astype(jnp.float32)
    for part in parts[1:]:
        total = total + part.astype(jnp.float32)
    return total.astype(parts[0].dtype)


def finish_kernel(own_ref, before_ref, after_ref, done_ref, out_ref):
    turn = lax.rem(lax.axis_index("rep"), SPLIT)
    rows = own_ref.shape[0]
    for shift, ref in ((0, own_ref), (SPLIT - 1, before_ref), (1, after_ref)):
        first = lax.rem(turn + shift, SPLIT) * rows
        for at in range(rows // BLOCK):
            tile = ref[at * BLOCK:(at + 1) * BLOCK, :].astype(out_ref.dtype)
            out_ref[pl.ds(pl.multiple_of(first + at * BLOCK, BLOCK), BLOCK), :] = tile.T


def finished(own, before, after, done):
    return pl.pallas_call(
        finish_kernel,
        in_specs=[pl.BlockSpec(memory_space=pltpu.VMEM)] * 3 + [pl.BlockSpec(memory_space=pl.ANY)],
        out_shape=jax.ShapeDtypeStruct((SPLIT * own.shape[0], own.shape[1]), jnp.float32),
        compiler_params=SMALL,
        name="finish_weight_grad",
    )(own, before, after, done)


def compact_kernel(slot_blocks, n_tp, blocks_ref, held_ref, grad_ref, *rest):
    outs, place = rest[:n_tp], rest[n_tp]
    index = lax.axis_index("tp")
    fill_places(blocks_ref, place, slot_blocks, lambda owner, at: (owner * slot_blocks + at) * PIECE)
    per = (outs[0].shape[0] - grad_ref.shape[0]) // PIECE
    for k, out_ref in enumerate(outs):
        first = lax.rem(index + k, n_tp) * per
        for at in range(per):
            source = pl.multiple_of(place[first + at], PIECE)
            out_ref[at * PIECE:(at + 1) * PIECE, :] = held_ref[pl.ds(source, PIECE), :]
        out_ref[per * PIECE:, :] = grad_ref[...]


def compacted(shard_blocks, held, grad, slot_rows, n_tp, width):
    n_blocks = width // BLOCK
    slot_blocks = slot_rows // BLOCK
    rows = n_blocks // n_tp * PIECE + grad.shape[0]
    vmem = pl.BlockSpec(memory_space=pltpu.VMEM)
    return pl.pallas_call(
        functools.partial(compact_kernel, slot_blocks, n_tp),
        in_specs=[pl.BlockSpec(memory_space=pltpu.SMEM), vmem, vmem],
        out_specs=[vmem] * n_tp,
        out_shape=[jax.ShapeDtypeStruct((rows, grad.shape[1]), grad.dtype)] * n_tp,
        scratch_shapes=[pltpu.SMEM((n_blocks + slot_blocks,), jnp.int32)],
        compiler_params=SMALL,
        cost_estimate=pl.CostEstimate(flops=0, bytes_accessed=2 * rows * grad.shape[1], transcendentals=0),
        name="compact_rows",
    )(shard_blocks, held, grad)


def stack_kernel(heads, *refs):
    own, out_ref = refs[:heads], refs[-1]
    for h in range(heads):
        out_ref[h] = own[h][: out_ref.shape[1], :]


def stacked(own, pieces, done):
    n, head = len(own), own[0].shape[1]
    vmem = pl.BlockSpec(memory_space=pltpu.VMEM)
    return pl.pallas_call(
        functools.partial(stack_kernel, n),
        in_specs=[vmem] * n + [pl.BlockSpec(memory_space=pl.ANY)],
        out_specs=vmem,
        out_shape=jax.ShapeDtypeStruct((n, pieces, head), own[0].dtype),
        compiler_params=SMALL,
        cost_estimate=pl.CostEstimate(flops=0, bytes_accessed=4 * n * pieces * head, transcendentals=0),
        name="stack_rows",
    )(*own, done)


def halve_kernel(own_ref, other_ref, *outs):
    half = own_ref.shape[0] // 2
    for k, out_ref in enumerate(outs):
        out_ref[:half] = own_ref[k * half:(k + 1) * half]
        out_ref[half:] = other_ref[k * half:(k + 1) * half]


def halved(own, other):
    vmem = pl.BlockSpec(memory_space=pltpu.VMEM)
    return pl.pallas_call(
        halve_kernel,
        in_specs=[vmem] * 2,
        out_specs=[vmem] * 2,
        out_shape=[jax.ShapeDtypeStruct(own.shape, own.dtype)] * 2,
        compiler_params=SMALL,
        cost_estimate=pl.CostEstimate(flops=0, bytes_accessed=8 * own.size, transcendentals=0),
        name="halve_heads",
    )(own, other)


def input_kernel(heads, counts_ref, own_ref, other_ref, *refs):
    far, grads = refs[:2], refs[2:heads + 2]
    out_ref, done_ref, masked, weight = refs[heads + 2:]
    turn = lax.rem(lax.axis_index("rep"), 2)
    core = lax.rem(lax.axis_index("dp"), 2)
    blocks = own_ref.shape[1] // PIECE
    half = heads // 2

    @pl.when(pl.program_id(0) == 0)
    def _():
        done_ref[...] = jnp.zeros_like(done_ref)
        for h in range(heads):
            grad = grads[h][...].astype(jnp.float32)
            live = lax.broadcasted_iota(jnp.int32, grad.shape, 0) < counts_ref[0]
            masked[:, h * BLOCK:(h + 1) * BLOCK] = jnp.where(live, grad, 0.0).astype(masked.dtype)

    for h in range(heads):
        sources = (
            (own_ref.at[h], turn, core),
            (other_ref.at[h], turn, 1 - core),
            (far[h // half].at[h % half], 1 - turn, core),
            (far[h // half].at[half + h % half], 1 - turn, 1 - core),
        )
        for ref, its_turn, its_core in sources:
            first = (2 * its_turn + its_core) * PIECE
            for b in range(blocks):
                rows = pl.ds(pl.multiple_of(b * BLOCK + first, PIECE), PIECE)
                weight[rows, h * BLOCK:(h + 1) * BLOCK] = ref[b * PIECE:(b + 1) * PIECE, :]

    out_ref[...] = lax.dot_general(
        masked[...], weight[...], (((1,), (1,)), ((), ())), preferred_element_type=jnp.float32
    ).astype(out_ref.dtype)


def input_product(counts, parts, own, other, far, rows_dev):
    n_tp, pieces, head = own.shape
    steps = 4
    blocks = pieces // PIECE // steps
    chunk = blocks * BLOCK
    piece = pl.BlockSpec((n_tp, blocks * PIECE, head), lambda i: (0, i, 0))
    return pl.pallas_call(
        functools.partial(input_kernel, n_tp),
        grid=(steps,),
        in_specs=[pl.BlockSpec(memory_space=pltpu.SMEM)]
        + [piece] * 4
        + [pl.BlockSpec((pl.Element(rows_dev), pl.Element(head)), lambda i: (pieces, 0))] * n_tp,
        out_specs=[
            pl.BlockSpec((rows_dev, chunk), lambda i: (0, i)),
            pl.BlockSpec((8, 128), lambda i: (0, 0)),
        ],
        out_shape=[
            jax.ShapeDtypeStruct((rows_dev, steps * chunk), jnp.bfloat16),
            jax.ShapeDtypeStruct((8, 128), jnp.float32),
        ],
        scratch_shapes=[
            pltpu.VMEM((rows_dev, head * n_tp), jnp.bfloat16),
            pltpu.VMEM((chunk, head * n_tp), jnp.bfloat16),
        ],
        compiler_params=pltpu.CompilerParams(vmem_limit_bytes=16 * 1024 * 1024),
        cost_estimate=pl.CostEstimate(
            flops=2 * rows_dev * steps * chunk * head * n_tp,
            bytes_accessed=2 * steps * chunk * (head * n_tp + rows_dev),
            transcendentals=0,
        ),
        name="input_grad",
    )(counts, own, other, *far, *parts)


def ordered(array, other):
    return lax.optimization_barrier((array, other))[0]


def on_device(hidden_in, value_grad, weight_shards, shard_blocks, token_counts):
    rows_dev, width = hidden_in.shape
    slot_rows, head = weight_shards.shape
    n_dp, n_tp, n_rep = lax.axis_size("dp"), lax.axis_size("tp"), lax.axis_size("rep")
    n_y = n_dp // 2
    slot_blocks = slot_rows // BLOCK
    core_swap = [(i, i ^ 1) for i in range(n_dp)]
    along_y = [[c + 2 * y for y in range(n_y)] for c in range(2)]
    up = [(i, (i + 1) % n_rep) for i in range(n_rep)]
    down = [(i, (i - 1) % n_rep) for i in range(n_rep)]

    turn = lax.rem(lax.axis_index("rep"), 2)
    halves = lax.dynamic_slice_in_dim(
        weight_shards.reshape(slot_blocks, BLOCK, head), 2 * turn * PIECE, 2 * PIECE, 1
    )
    quarters = halves.reshape(slot_blocks, 2, PIECE, head).swapaxes(0, 1).reshape(1, 2, slot_blocks * PIECE, head)
    held = lax.all_to_all(
        jnp.broadcast_to(quarters, (n_y,) + quarters.shape[1:]).reshape(n_dp, slot_blocks * PIECE, head), "dp", 0, 0
    ).reshape(n_dp * slot_blocks * PIECE, head)
    send, keep = grad_products(token_counts, shard_blocks, hidden_in, value_grad, slot_rows)
    received = lax.ppermute(send, "dp", core_swap)
    third = send.shape[0] // SPLIT
    stay, to_next, to_last = (
        summed([half[k * third:(k + 1) * third] for half in (keep, received)]) for k in range(SPLIT)
    )

    part = summed([stay, lax.ppermute(to_next, "rep", up), lax.ppermute(to_last, "rep", down)])
    held = ordered(held, part)
    sent = compacted(shard_blocks, held, value_grad, slot_rows, n_tp, width)
    parts = [sent[0]] + [
        lax.ppermute(sent[k], "tp", [(i, (i + k) % n_tp) for i in range(n_tp)]) for k in range(1, n_tp)
    ]

    spread = lax.all_to_all(part.reshape(n_y, slot_rows // SPLIT, head), "dp", 0, 0, axis_index_groups=along_y)
    owned = summed([spread[y] for y in range(n_y)])
    own = stacked(parts, parts[0].shape[0] - rows_dev, spread)
    other = lax.ppermute(own, "dp", core_swap)
    first, second = halved(own, other)
    far = [lax.ppermute(first, "rep", up), lax.ppermute(second, "rep", down)]
    input_grad, done = input_product(token_counts, parts, own, other, far, rows_dev)

    n_fellows = n_rep // SPLIT
    fellows = [[k + SPLIT * q for q in range(n_fellows)] for k in range(SPLIT)]
    shares = lax.all_to_all(
        jnp.broadcast_to(owned[None], (n_fellows,) + owned.shape), "rep", 0, 0, axis_index_groups=fellows
    )
    third = summed([shares[q] for q in range(n_fellows)])
    weight_grad = finished(third, lax.ppermute(third, "rep", up), lax.ppermute(third, "rep", down), done)
    return (input_grad, weight_grad)


def solution(mesh):
    placed = (P(("rep", "dp"), None), P(("rep", "dp"), "tp"), P("dp", "tp"), P(), P(("rep", "dp")))
    return jax.shard_map(
        on_device,
        mesh=mesh,
        in_specs=placed,
        out_specs=(P(("rep", "dp"), "tp"), P("dp", "tp")),
        check_vma=False,
    )
```

```python
import functools

import jax
import jax.numpy as jnp
from jax import lax
from jax.experimental import pallas as pl
from jax.experimental.pallas import tpu as pltpu
from jax.sharding import PartitionSpec as P

BLOCK = 128
SPLIT = 3
AHEAD = 3
PIECE = 32
SMALL = pltpu.CompilerParams(vmem_limit_bytes=12 * 1024 * 1024)


def fill_places(blocks_ref, place, slot_blocks, code):
    first = 0
    for owner in range(blocks_ref.shape[0]):
        for at in range(slot_blocks):
            place[first + at] = code(owner, at)
        first = first + blocks_ref[owner]


def grad_kernel(
    chunk, slot_blocks, counts_ref, blocks_ref, hidden_ref, grad_ref, send_ref, keep_ref, place, masked_t, chunks, sems
):
    steps = hidden_ref.shape[1] // chunk

    def load(step):
        return pltpu.make_async_copy(
            hidden_ref.at[:, pl.ds(step * chunk, chunk)], chunks.at[step], sems.at[step]
        )

    for step in range(min(AHEAD, steps)):
        load(step).start()
    core = lax.rem(lax.axis_index("dp"), 2)
    turn = lax.rem(lax.axis_index("rep"), SPLIT)
    half = send_ref.shape[0]
    part_blocks = slot_blocks // SPLIT
    part_first = [lax.rem(part + SPLIT - turn, SPLIT) * (half // SPLIT) for part in range(SPLIT)]
    side = [jnp.where(core == parity, 0, half) for parity in range(2)]

    def code(owner, at):
        row = ((owner // 2) * part_blocks + at % part_blocks) * BLOCK
        return part_first[at // part_blocks] + side[owner % 2] + row

    fill_places(blocks_ref, place, slot_blocks, code)
    send_ref[...] = jnp.zeros_like(send_ref)
    keep_ref[...] = jnp.zeros_like(keep_ref)
    live = lax.broadcasted_iota(jnp.int32, grad_ref.shape, 0) < counts_ref[0]
    masked = jnp.where(live, grad_ref[...].astype(jnp.float32), 0.0)
    masked_t[...] = masked.T.astype(masked_t.dtype)

    def one(step, carry):
        load(step).wait()

        @pl.when(step + AHEAD < steps)
        def _():
            load(step + AHEAD).start()

        product = jnp.dot(masked_t[...], chunks[step], preferred_element_type=jnp.float32)
        for at in range(chunk // BLOCK):
            row = place[step * (chunk // BLOCK) + at]
            tile = product[:, at * BLOCK:(at + 1) * BLOCK].astype(send_ref.dtype)

            @pl.when(row < half)
            def _():
                keep_ref[pl.ds(pl.multiple_of(row, BLOCK), BLOCK), :] = tile

            @pl.when(row >= half)
            def _():
                send_ref[pl.ds(pl.multiple_of(row - half, BLOCK), BLOCK), :] = tile

        return carry

    lax.fori_loop(0, steps, one, 0)


def grad_products(counts, shard_blocks, hidden, grad, slot_rows):
    rows, width = hidden.shape
    owners = shard_blocks.shape[0]
    chunk = 1024
    steps = width // chunk
    half = (owners // 2) * slot_rows
    slot_blocks = slot_rows // BLOCK
    out = jax.ShapeDtypeStruct((half, grad.shape[1]), jnp.bfloat16)
    vmem = pl.BlockSpec(memory_space=pltpu.VMEM)
    return pl.pallas_call(
        functools.partial(grad_kernel, chunk, slot_blocks),
        in_specs=[
            pl.BlockSpec(memory_space=pltpu.SMEM),
            pl.BlockSpec(memory_space=pltpu.SMEM),
            pl.BlockSpec(memory_space=pltpu.HBM),
            vmem,
        ],
        out_specs=[vmem, vmem],
        out_shape=[out, out],
        scratch_shapes=[
            pltpu.SMEM((width // BLOCK + slot_blocks,), jnp.int32),
            pltpu.VMEM((grad.shape[1], rows), jnp.bfloat16),
            pltpu.VMEM((steps, rows, chunk), jnp.bfloat16),
            pltpu.SemaphoreType.DMA((steps,)),
        ],
        compiler_params=pltpu.CompilerParams(vmem_limit_bytes=59 * 1024 * 1024),
        cost_estimate=pl.CostEstimate(
            flops=2 * rows * width * grad.shape[1], bytes_accessed=2 * rows * width + 4 * half * 128, transcendentals=0
        ),
        name="grad_products",
    )(counts, shard_blocks, hidden, grad)


def summed(parts):
    total = parts[0].astype(jnp.float32)
    for part in parts[1:]:
        total = total + part.astype(jnp.float32)
    return total.astype(parts[0].dtype)


def finish_kernel(own_ref, before_ref, after_ref, done_ref, out_ref):
    turn = lax.rem(lax.axis_index("rep"), SPLIT)
    rows = own_ref.shape[0]
    for shift, ref in ((0, own_ref), (SPLIT - 1, before_ref), (1, after_ref)):
        first = lax.rem(turn + shift, SPLIT) * rows
        for at in range(rows // BLOCK):
            tile = ref[at * BLOCK:(at + 1) * BLOCK, :].astype(out_ref.dtype)
            out_ref[pl.ds(pl.multiple_of(first + at * BLOCK, BLOCK), BLOCK), :] = tile.T


def finished(own, before, after, done):
    return pl.pallas_call(
        finish_kernel,
        in_specs=[pl.BlockSpec(memory_space=pltpu.VMEM)] * 3 + [pl.BlockSpec(memory_space=pl.ANY)],
        out_shape=jax.ShapeDtypeStruct((SPLIT * own.shape[0], own.shape[1]), jnp.float32),
        compiler_params=SMALL,
        name="finish_weight_grad",
    )(own, before, after, done)


def compact_kernel(slot_blocks, n_tp, blocks_ref, held_ref, grad_ref, *rest):
    outs, place = rest[:n_tp], rest[n_tp]
    index = lax.axis_index("tp")
    fill_places(blocks_ref, place, slot_blocks, lambda owner, at: (owner * slot_blocks + at) * PIECE)
    per = (outs[0].shape[0] - grad_ref.shape[0]) // PIECE
    for k, out_ref in enumerate(outs):
        first = lax.rem(index + k, n_tp) * per
        for at in range(per):
            source = pl.multiple_of(place[first + at], PIECE)
            out_ref[at * PIECE:(at + 1) * PIECE, :] = held_ref[pl.ds(source, PIECE), :]
        out_ref[per * PIECE:, :] = grad_ref[...]


def compacted(shard_blocks, held, grad, slot_rows, n_tp, width):
    n_blocks = width // BLOCK
    slot_blocks = slot_rows // BLOCK
    rows = n_blocks // n_tp * PIECE + grad.shape[0]
    vmem = pl.BlockSpec(memory_space=pltpu.VMEM)
    return pl.pallas_call(
        functools.partial(compact_kernel, slot_blocks, n_tp),
        in_specs=[pl.BlockSpec(memory_space=pltpu.SMEM), vmem, vmem],
        out_specs=[vmem] * n_tp,
        out_shape=[jax.ShapeDtypeStruct((rows, grad.shape[1]), grad.dtype)] * n_tp,
        scratch_shapes=[pltpu.SMEM((n_blocks + slot_blocks,), jnp.int32)],
        compiler_params=SMALL,
        cost_estimate=pl.CostEstimate(flops=0, bytes_accessed=2 * rows * grad.shape[1], transcendentals=0),
        name="compact_rows",
    )(shard_blocks, held, grad)


def stack_kernel(heads, *refs):
    own, outs = refs[:heads], refs[-2:]
    half = heads // 2
    for h in range(heads):
        outs[h // half][h % half] = own[h][: outs[0].shape[1], :]


def stacked(own, pieces, done):
    n, head = len(own), own[0].shape[1]
    vmem = pl.BlockSpec(memory_space=pltpu.VMEM)
    return pl.pallas_call(
        functools.partial(stack_kernel, n),
        in_specs=[vmem] * n + [pl.BlockSpec(memory_space=pl.ANY)],
        out_specs=[vmem] * 2,
        out_shape=[jax.ShapeDtypeStruct((n // 2, pieces, head), own[0].dtype)] * 2,
        compiler_params=SMALL,
        cost_estimate=pl.CostEstimate(flops=0, bytes_accessed=4 * n * pieces * head, transcendentals=0),
        name="stack_rows",
    )(*own, done)


def input_kernel(heads, counts_ref, *refs):
    own, other, far, far_other = refs[:2], refs[2:4], refs[4:6], refs[6:8]
    grads = refs[8:heads + 8]
    out_ref, done_ref, masked, weight = refs[heads + 8:]
    turn = lax.rem(lax.axis_index("rep"), 2)
    core = lax.rem(lax.axis_index("dp"), 2)
    blocks = own[0].shape[1] // PIECE
    half = heads // 2

    @pl.when(pl.program_id(0) == 0)
    def _():
        done_ref[...] = jnp.zeros_like(done_ref)
        for h in range(heads):
            grad = grads[h][...].astype(jnp.float32)
            live = lax.broadcasted_iota(jnp.int32, grad.shape, 0) < counts_ref[0]
            masked[:, h * BLOCK:(h + 1) * BLOCK] = jnp.where(live, grad, 0.0).astype(masked.dtype)

    for h in range(heads):
        part, at = h // half, h % half
        sources = (
            (own[part].at[at], turn, core),
            (other[part].at[at], turn, 1 - core),
            (far[part].at[at], 1 - turn, core),
            (far_other[part].at[at], 1 - turn, 1 - core),
        )
        for ref, its_turn, its_core in sources:
            first = (2 * its_turn + its_core) * PIECE
            for b in range(blocks):
                rows = pl.ds(pl.multiple_of(b * BLOCK + first, PIECE), PIECE)
                weight[rows, h * BLOCK:(h + 1) * BLOCK] = ref[b * PIECE:(b + 1) * PIECE, :]

    out_ref[...] = lax.dot_general(
        masked[...], weight[...], (((1,), (1,)), ((), ())), preferred_element_type=jnp.float32
    ).astype(out_ref.dtype)


def input_product(counts, parts, own, other, far, far_other, rows_dev):
    n_tp = len(parts)
    _, pieces, head = own[0].shape
    steps = 4
    blocks = pieces // PIECE // steps
    chunk = blocks * BLOCK
    piece = pl.BlockSpec((n_tp // 2, blocks * PIECE, head), lambda i: (0, i, 0))
    return pl.pallas_call(
        functools.partial(input_kernel, n_tp),
        grid=(steps,),
        in_specs=[pl.BlockSpec(memory_space=pltpu.SMEM)]
        + [piece] * 8
        + [pl.BlockSpec((pl.Element(rows_dev), pl.Element(head)), lambda i: (pieces, 0))] * n_tp,
        out_specs=[
            pl.BlockSpec((rows_dev, chunk), lambda i: (0, i)),
            pl.BlockSpec((8, 128), lambda i: (0, 0)),
        ],
        out_shape=[
            jax.ShapeDtypeStruct((rows_dev, steps * chunk), jnp.bfloat16),
            jax.ShapeDtypeStruct((8, 128), jnp.float32),
        ],
        scratch_shapes=[
            pltpu.VMEM((rows_dev, head * n_tp), jnp.bfloat16),
            pltpu.VMEM((chunk, head * n_tp), jnp.bfloat16),
        ],
        compiler_params=pltpu.CompilerParams(vmem_limit_bytes=16 * 1024 * 1024),
        cost_estimate=pl.CostEstimate(
            flops=2 * rows_dev * steps * chunk * head * n_tp,
            bytes_accessed=2 * steps * chunk * (head * n_tp + rows_dev),
            transcendentals=0,
        ),
        name="input_grad",
    )(counts, *own, *other, *far, *far_other, *parts)


def ordered(array, other):
    return lax.optimization_barrier((array, other))[0]


def on_device(hidden_in, value_grad, weight_shards, shard_blocks, token_counts):
    rows_dev, width = hidden_in.shape
    slot_rows, head = weight_shards.shape
    n_dp, n_tp, n_rep = lax.axis_size("dp"), lax.axis_size("tp"), lax.axis_size("rep")
    n_y = n_dp // 2
    slot_blocks = slot_rows // BLOCK
    core_swap = [(i, i ^ 1) for i in range(n_dp)]
    along_y = [[c + 2 * y for y in range(n_y)] for c in range(2)]
    up = [(i, (i + 1) % n_rep) for i in range(n_rep)]
    down = [(i, (i - 1) % n_rep) for i in range(n_rep)]

    turn = lax.rem(lax.axis_index("rep"), 2)
    halves = lax.dynamic_slice_in_dim(
        weight_shards.reshape(slot_blocks, BLOCK, head), 2 * turn * PIECE, 2 * PIECE, 1
    )
    quarters = halves.reshape(slot_blocks, 2, PIECE, head).swapaxes(0, 1).reshape(1, 2, slot_blocks * PIECE, head)
    held = lax.all_to_all(
        jnp.broadcast_to(quarters, (n_y,) + quarters.shape[1:]).reshape(n_dp, slot_blocks * PIECE, head), "dp", 0, 0
    ).reshape(n_dp * slot_blocks * PIECE, head)
    send, keep = grad_products(token_counts, shard_blocks, hidden_in, value_grad, slot_rows)
    received = lax.ppermute(send, "dp", core_swap)
    third = send.shape[0] // SPLIT
    stay, to_next, to_last = (
        summed([half[k * third:(k + 1) * third] for half in (keep, received)]) for k in range(SPLIT)
    )

    part = summed([stay, lax.ppermute(to_next, "rep", up), lax.ppermute(to_last, "rep", down)])
    held = ordered(held, part)
    sent = compacted(shard_blocks, held, value_grad, slot_rows, n_tp, width)
    parts = [sent[0]] + [
        lax.ppermute(sent[k], "tp", [(i, (i + k) % n_tp) for i in range(n_tp)]) for k in range(1, n_tp)
    ]

    spread = lax.all_to_all(part.reshape(n_y, slot_rows // SPLIT, head), "dp", 0, 0, axis_index_groups=along_y)
    spread = ordered(spread, parts)
    owned = summed([spread[y] for y in range(n_y)])
    own = stacked(parts, parts[0].shape[0] - rows_dev, spread)
    other = [lax.ppermute(part, "dp", core_swap) for part in own]
    far = [lax.ppermute(own[0], "rep", up), lax.ppermute(own[1], "rep", down)]
    far_other = [lax.ppermute(part, "dp", core_swap) for part in far]
    input_grad, done = input_product(token_counts, parts, own, other, far, far_other, rows_dev)

    n_fellows = n_rep // SPLIT
    fellows = [[k + SPLIT * q for q in range(n_fellows)] for k in range(SPLIT)]
    shares = lax.all_to_all(
        jnp.broadcast_to(owned[None], (n_fellows,) + owned.shape), "rep", 0, 0, axis_index_groups=fellows
    )
    third = summed([shares[q] for q in range(n_fellows)])
    weight_grad = finished(third, lax.ppermute(third, "rep", up), lax.ppermute(third, "rep", down), done)
    return (input_grad, weight_grad)


def solution(mesh):
    placed = (P(("rep", "dp"), None), P(("rep", "dp"), "tp"), P("dp", "tp"), P(), P(("rep", "dp")))
    return jax.shard_map(
        on_device,
        mesh=mesh,
        in_specs=placed,
        out_specs=(P(("rep", "dp"), "tp"), P("dp", "tp")),
        check_vma=False,
    )
```

```python
import functools

import jax
import jax.numpy as jnp
from jax import lax
from jax.experimental import pallas as pl
from jax.experimental.pallas import tpu as pltpu
from jax.sharding import PartitionSpec as P

BLOCK = 128
SPLIT = 3
AHEAD = 3
PIECE = 32
SMALL = pltpu.CompilerParams(vmem_limit_bytes=12 * 1024 * 1024)


def fill_places(blocks_ref, place, slot_blocks, code):
    first = 0
    for owner in range(blocks_ref.shape[0]):
        for at in range(slot_blocks):
            place[first + at] = code(owner, at)
        first = first + blocks_ref[owner]


def grad_kernel(
    chunk, slot_blocks, counts_ref, blocks_ref, hidden_ref, grad_ref, send_ref, keep_ref, place, masked_t, chunks, sems
):
    steps = hidden_ref.shape[1] // chunk

    def load(step):
        return pltpu.make_async_copy(
            hidden_ref.at[:, pl.ds(step * chunk, chunk)], chunks.at[step], sems.at[step]
        )

    for step in range(min(AHEAD, steps)):
        load(step).start()
    core = lax.rem(lax.axis_index("dp"), 2)
    turn = lax.rem(lax.axis_index("rep"), SPLIT)
    half = send_ref.shape[0]
    part_blocks = slot_blocks // SPLIT
    part_first = [lax.rem(part + SPLIT - turn, SPLIT) * (half // SPLIT) for part in range(SPLIT)]
    side = [jnp.where(core == parity, 0, half) for parity in range(2)]

    def code(owner, at):
        row = ((owner // 2) * part_blocks + at % part_blocks) * BLOCK
        return part_first[at // part_blocks] + side[owner % 2] + row

    fill_places(blocks_ref, place, slot_blocks, code)
    send_ref[...] = jnp.zeros_like(send_ref)
    keep_ref[...] = jnp.zeros_like(keep_ref)
    live = lax.broadcasted_iota(jnp.int32, grad_ref.shape, 0) < counts_ref[0]
    masked = jnp.where(live, grad_ref[...].astype(jnp.float32), 0.0)
    masked_t[...] = masked.T.astype(masked_t.dtype)

    def one(step, carry):
        load(step).wait()

        @pl.when(step + AHEAD < steps)
        def _():
            load(step + AHEAD).start()

        product = jnp.dot(masked_t[...], chunks[step], preferred_element_type=jnp.float32)
        for at in range(chunk // BLOCK):
            row = place[step * (chunk // BLOCK) + at]
            tile = product[:, at * BLOCK:(at + 1) * BLOCK].astype(send_ref.dtype)

            @pl.when(row < half)
            def _():
                keep_ref[pl.ds(pl.multiple_of(row, BLOCK), BLOCK), :] = tile

            @pl.when(row >= half)
            def _():
                send_ref[pl.ds(pl.multiple_of(row - half, BLOCK), BLOCK), :] = tile

        return carry

    lax.fori_loop(0, steps, one, 0)


def grad_products(counts, shard_blocks, hidden, grad, slot_rows):
    rows, width = hidden.shape
    owners = shard_blocks.shape[0]
    chunk = 1024
    steps = width // chunk
    half = (owners // 2) * slot_rows
    slot_blocks = slot_rows // BLOCK
    out = jax.ShapeDtypeStruct((half, grad.shape[1]), jnp.bfloat16)
    vmem = pl.BlockSpec(memory_space=pltpu.VMEM)
    return pl.pallas_call(
        functools.partial(grad_kernel, chunk, slot_blocks),
        in_specs=[
            pl.BlockSpec(memory_space=pltpu.SMEM),
            pl.BlockSpec(memory_space=pltpu.SMEM),
            pl.BlockSpec(memory_space=pltpu.HBM),
            vmem,
        ],
        out_specs=[vmem, vmem],
        out_shape=[out, out],
        scratch_shapes=[
            pltpu.SMEM((width // BLOCK + slot_blocks,), jnp.int32),
            pltpu.VMEM((grad.shape[1], rows), jnp.bfloat16),
            pltpu.VMEM((steps, rows, chunk), jnp.bfloat16),
            pltpu.SemaphoreType.DMA((steps,)),
        ],
        compiler_params=pltpu.CompilerParams(vmem_limit_bytes=59 * 1024 * 1024),
        cost_estimate=pl.CostEstimate(
            flops=2 * rows * width * grad.shape[1], bytes_accessed=2 * rows * width + 4 * half * 128, transcendentals=0
        ),
        name="grad_products",
    )(counts, shard_blocks, hidden, grad)


def summed(parts):
    total = parts[0].astype(jnp.float32)
    for part in parts[1:]:
        total = total + part.astype(jnp.float32)
    return total.astype(parts[0].dtype)


def finish_kernel(own_ref, before_ref, after_ref, out_ref):
    turn = lax.rem(lax.axis_index("rep"), SPLIT)
    rows = own_ref.shape[0]
    for shift, ref in ((0, own_ref), (SPLIT - 1, before_ref), (1, after_ref)):
        first = lax.rem(turn + shift, SPLIT) * rows
        for at in range(rows // BLOCK):
            tile = ref[at * BLOCK:(at + 1) * BLOCK, :].astype(out_ref.dtype)
            out_ref[pl.ds(pl.multiple_of(first + at * BLOCK, BLOCK), BLOCK), :] = tile.T


def finished(own, before, after):
    return pl.pallas_call(
        finish_kernel,
        out_shape=jax.ShapeDtypeStruct((SPLIT * own.shape[0], own.shape[1]), jnp.float32),
        compiler_params=SMALL,
        name="finish_weight_grad",
    )(own, before, after)


def compact_kernel(slot_blocks, n_tp, blocks_ref, held_ref, grad_ref, *rest):
    outs, place = rest[:n_tp], rest[n_tp]
    index = lax.axis_index("tp")
    fill_places(blocks_ref, place, slot_blocks, lambda owner, at: (owner * slot_blocks + at) * PIECE)
    per = (outs[0].shape[0] - grad_ref.shape[0]) // PIECE
    for k, out_ref in enumerate(outs):
        first = lax.rem(index + k, n_tp) * per
        for at in range(per):
            source = pl.multiple_of(place[first + at], PIECE)
            out_ref[at * PIECE:(at + 1) * PIECE, :] = held_ref[pl.ds(source, PIECE), :]
        out_ref[per * PIECE:, :] = grad_ref[...]


def compacted(shard_blocks, held, grad, slot_rows, n_tp, width):
    n_blocks = width // BLOCK
    slot_blocks = slot_rows // BLOCK
    rows = n_blocks // n_tp * PIECE + grad.shape[0]
    vmem = pl.BlockSpec(memory_space=pltpu.VMEM)
    return pl.pallas_call(
        functools.partial(compact_kernel, slot_blocks, n_tp),
        in_specs=[pl.BlockSpec(memory_space=pltpu.SMEM), vmem, vmem],
        out_specs=[vmem] * n_tp,
        out_shape=[jax.ShapeDtypeStruct((rows, grad.shape[1]), grad.dtype)] * n_tp,
        scratch_shapes=[pltpu.SMEM((n_blocks + slot_blocks,), jnp.int32)],
        compiler_params=SMALL,
        cost_estimate=pl.CostEstimate(flops=0, bytes_accessed=2 * rows * grad.shape[1], transcendentals=0),
        name="compact_rows",
    )(shard_blocks, held, grad)


def stack_kernel(heads, *refs):
    own, out_ref = refs[:heads], refs[-1]
    for h in range(heads):
        out_ref[h] = own[h][: out_ref.shape[1], :]


def stacked(own, pieces, done):
    n, head = len(own), own[0].shape[1]
    vmem = pl.BlockSpec(memory_space=pltpu.VMEM)
    return pl.pallas_call(
        functools.partial(stack_kernel, n),
        in_specs=[vmem] * n + [pl.BlockSpec(memory_space=pl.ANY)],
        out_specs=vmem,
        out_shape=jax.ShapeDtypeStruct((n, pieces, head), own[0].dtype),
        compiler_params=SMALL,
        cost_estimate=pl.CostEstimate(flops=0, bytes_accessed=4 * n * pieces * head, transcendentals=0),
        name="stack_rows",
    )(*own, done)


def halve_kernel(own_ref, other_ref, *outs):
    half = own_ref.shape[0] // 2
    for k, out_ref in enumerate(outs):
        out_ref[:half] = own_ref[k * half:(k + 1) * half]
        out_ref[half:] = other_ref[k * half:(k + 1) * half]


def halved(own, other):
    vmem = pl.BlockSpec(memory_space=pltpu.VMEM)
    return pl.pallas_call(
        halve_kernel,
        in_specs=[vmem] * 2,
        out_specs=[vmem] * 2,
        out_shape=[jax.ShapeDtypeStruct(own.shape, own.dtype)] * 2,
        compiler_params=SMALL,
        cost_estimate=pl.CostEstimate(flops=0, bytes_accessed=8 * own.size, transcendentals=0),
        name="halve_heads",
    )(own, other)


def input_kernel(heads, counts_ref, own_ref, other_ref, *refs):
    far, grads = refs[:2], refs[2:heads + 2]
    out_ref, masked, weight = refs[heads + 2:]
    turn = lax.rem(lax.axis_index("rep"), 2)
    core = lax.rem(lax.axis_index("dp"), 2)
    blocks = own_ref.shape[1] // PIECE
    half = heads // 2

    @pl.when(pl.program_id(0) == 0)
    def _():
        for h in range(heads):
            grad = grads[h][...].astype(jnp.float32)
            live = lax.broadcasted_iota(jnp.int32, grad.shape, 0) < counts_ref[0]
            masked[:, h * BLOCK:(h + 1) * BLOCK] = jnp.where(live, grad, 0.0).astype(masked.dtype)

    for h in range(heads):
        sources = (
            (own_ref.at[h], turn, core),
            (other_ref.at[h], turn, 1 - core),
            (far[h // half].at[h % half], 1 - turn, core),
            (far[h // half].at[half + h % half], 1 - turn, 1 - core),
        )
        for ref, its_turn, its_core in sources:
            first = (2 * its_turn + its_core) * PIECE
            for b in range(blocks):
                rows = pl.ds(pl.multiple_of(b * BLOCK + first, PIECE), PIECE)
                weight[rows, h * BLOCK:(h + 1) * BLOCK] = ref[b * PIECE:(b + 1) * PIECE, :]

    out_ref[...] = lax.dot_general(
        masked[...], weight[...], (((1,), (1,)), ((), ())), preferred_element_type=jnp.float32
    ).astype(out_ref.dtype)


def input_product(counts, parts, own, other, far, rows_dev):
    n_tp, pieces, head = own.shape
    steps = 4
    blocks = pieces // PIECE // steps
    chunk = blocks * BLOCK
    piece = pl.BlockSpec((n_tp, blocks * PIECE, head), lambda i: (0, i, 0))
    return pl.pallas_call(
        functools.partial(input_kernel, n_tp),
        grid=(steps,),
        in_specs=[pl.BlockSpec(memory_space=pltpu.SMEM)]
        + [piece] * 4
        + [pl.BlockSpec((pl.Element(rows_dev), pl.Element(head)), lambda i: (pieces, 0))] * n_tp,
        out_specs=pl.BlockSpec((rows_dev, chunk), lambda i: (0, i)),
        out_shape=jax.ShapeDtypeStruct((rows_dev, steps * chunk), jnp.bfloat16),
        scratch_shapes=[
            pltpu.VMEM((rows_dev, head * n_tp), jnp.bfloat16),
            pltpu.VMEM((chunk, head * n_tp), jnp.bfloat16),
        ],
        compiler_params=pltpu.CompilerParams(vmem_limit_bytes=16 * 1024 * 1024),
        cost_estimate=pl.CostEstimate(
            flops=2 * rows_dev * steps * chunk * head * n_tp,
            bytes_accessed=2 * steps * chunk * (head * n_tp + rows_dev),
            transcendentals=0,
        ),
        name="input_grad",
    )(counts, own, other, *far, *parts)


def ordered(array, other):
    return lax.optimization_barrier((array, other))[0]


def on_device(hidden_in, value_grad, weight_shards, shard_blocks, token_counts):
    rows_dev, width = hidden_in.shape
    slot_rows, head = weight_shards.shape
    n_dp, n_tp, n_rep = lax.axis_size("dp"), lax.axis_size("tp"), lax.axis_size("rep")
    n_y = n_dp // 2
    slot_blocks = slot_rows // BLOCK
    core_swap = [(i, i ^ 1) for i in range(n_dp)]
    along_y = [[c + 2 * y for y in range(n_y)] for c in range(2)]
    up = [(i, (i + 1) % n_rep) for i in range(n_rep)]
    down = [(i, (i - 1) % n_rep) for i in range(n_rep)]

    turn = lax.rem(lax.axis_index("rep"), 2)
    halves = lax.dynamic_slice_in_dim(
        weight_shards.reshape(slot_blocks, BLOCK, head), 2 * turn * PIECE, 2 * PIECE, 1
    )
    quarters = halves.reshape(slot_blocks, 2, PIECE, head).swapaxes(0, 1).reshape(1, 2, slot_blocks * PIECE, head)
    held = lax.all_to_all(
        jnp.broadcast_to(quarters, (n_y,) + quarters.shape[1:]).reshape(n_dp, slot_blocks * PIECE, head), "dp", 0, 0
    ).reshape(n_dp * slot_blocks * PIECE, head)
    send, keep = grad_products(token_counts, shard_blocks, hidden_in, value_grad, slot_rows)
    received = lax.ppermute(send, "dp", core_swap)
    third = send.shape[0] // SPLIT
    stay, to_next, to_last = (
        summed([half[k * third:(k + 1) * third] for half in (keep, received)]) for k in range(SPLIT)
    )

    part = summed([stay, lax.ppermute(to_next, "rep", up), lax.ppermute(to_last, "rep", down)])
    held = ordered(held, part)
    sent = compacted(shard_blocks, held, value_grad, slot_rows, n_tp, width)
    parts = [sent[0]] + [
        lax.ppermute(sent[k], "tp", [(i, (i + k) % n_tp) for i in range(n_tp)]) for k in range(1, n_tp)
    ]

    spread = lax.all_to_all(part.reshape(n_y, slot_rows // SPLIT, head), "dp", 0, 0, axis_index_groups=along_y)
    owned = summed([spread[y] for y in range(n_y)])
    own = stacked(parts, parts[0].shape[0] - rows_dev, spread)
    other = lax.ppermute(own, "dp", core_swap)
    first, second = halved(own, other)
    far = [lax.ppermute(first, "rep", up), lax.ppermute(second, "rep", down)]
    input_grad = input_product(token_counts, parts, own, other, far, rows_dev)

    n_fellows = n_rep // SPLIT
    fellows = [[k + SPLIT * q for q in range(n_fellows)] for k in range(SPLIT)]
    shares = lax.all_to_all(
        jnp.broadcast_to(owned[None], (n_fellows,) + owned.shape), "rep", 0, 0, axis_index_groups=fellows
    )
    third = summed([shares[q] for q in range(n_fellows)])
    weight_grad = finished(third, lax.ppermute(third, "rep", up), lax.ppermute(third, "rep", down))
    return (input_grad, weight_grad)


def solution(mesh):
    placed = (P(("rep", "dp"), None), P(("rep", "dp"), "tp"), P("dp", "tp"), P(), P(("rep", "dp")))
    return jax.shard_map(
        on_device,
        mesh=mesh,
        in_specs=placed,
        out_specs=(P(("rep", "dp"), "tp"), P("dp", "tp")),
        check_vma=False,
    )
```
